128 devices in a mesh: space: 16 (over x_lo, z, core), subj: 8 (over y, x_hi).
Axes of the slice: x: 4 (x_hi: 2, x_lo: 2; x = x_hi * 2 + x_lo), y: 4, z: 4, core: 2. Of those that a mesh axis runs over, the one named last changes fastest.
Arguments:
- template: float32 [128, 64, 256], P('space', 'subj'), may hold values from -6 to 6
- momentum: float32 [32, 3, 128, 64, 256], P('subj', None, 'space'), may hold values from -6 to 6
- targets: float32 [32, 128, 64, 256], P('subj', 'space'), may hold values from -6 to 6
- step_count: int32 [32], P('subj'), may hold values from 1 to 4, as said below
Outputs:
- warped: float32 [32, 128, 64, 256], P('subj', 'space')
- template_gradient: float32 [128, 64, 256], P('space', 'subj')
- momentum_gradient: float32 [32, 3, 128, 64, 256], P('subj', None, 'space')
The draws below stay inside these ranges and needn't reach their ends.
Inputs may be any that keep to these rules, and one draw needn't show every extreme that they name: `step_count`: each subject takes between 1 and 4 steps; some subject takes 4 and some takes 1.
All inputs are finite; a program needn't handle non-finite values.
Results may differ from the reference program's by a relative error of at most 0.0003.
Values sent between devices are 32-bit elements; how exact they have to be, the bound alone decides.
No kernel may reach another device: no remote copies, remote signals or barrier semaphores. Data moves between devices by JAX's collectives and lax.ppermute only.
A program may use at most 192 MiB of HBM per device.

```python
import jax
import jax.numpy as jnp
from jax import lax

NY = 64
NX = 256
STEPS = 4
NZ = 128
SUBJECTS = 32


def draw_step_count(key, part):
    key = jax.random.fold_in(key, 7)
    first, second = jax.random.split(key)
    counts = jax.random.randint(first, (SUBJECTS,), 1, STEPS + 1)
    where = jax.random.randint(second, (), 0, SUBJECTS)
    counts = counts.at[where].set(STEPS)
    counts = counts.at[(where + 1) % SUBJECTS].set(1)
    return counts.astype(jnp.int32)


def levels(key, dims, cuts, low, largest):
    def one(position, blocks):
        heights = jax.random.uniform(jax.random.fold_in(jax.random.fold_in(key, 6), position), (blocks,), jnp.float32, low / len(cuts), largest / len(cuts))
        return jnp.repeat(jnp.exp(heights), dims[position] // blocks).reshape((-1,) + (1,) * (len(dims) - position - 1))

    factor_of = one(*cuts[0])
    for cut in cuts[1:]:
        factor_of = factor_of * one(*cut)
    return factor_of


def centred(stream_key, extent, spread, most, pieces=(), dtype=jnp.bfloat16):
    values = spread * jax.random.normal(stream_key, extent, jnp.float32)
    if pieces:
        values = values * levels(stream_key, extent, pieces, -0.22, 0.18)
    return jnp.clip(values, -most, most).astype(dtype)


def setup_inputs(seed: int = 0) -> dict:
    arg_keys = jax.random.split(jax.random.key(seed), 5)
    return {
        "template": centred(arg_keys[0], (NZ, NY, NX), 1.0, 6.0, ((0, 16), (1, 8)), jnp.float32),
        "momentum": centred(arg_keys[1], (SUBJECTS, 3, NZ, NY, NX), 1.0, 6.0, ((0, 8), (2, 16)), jnp.float32),
        "targets": centred(arg_keys[2], (SUBJECTS, NZ, NY, NX), 1.0, 6.0, ((0, 8), (1, 16)), jnp.float32),
        "step_count": draw_step_count(jax.random.fold_in(arg_keys[4], 71), 0),
    }


time_step = 0.15
smoothing = 0.1

def central(field, axis):
    size = field.shape[axis]
    widths = [(0, 0)] * field.ndim
    widths[axis] = (1, 1)
    padded = jnp.pad(field, widths)
    upper = lax.slice_in_dim(padded, 2, size + 2, axis=axis)
    lower = lax.slice_in_dim(padded, 0, size, axis=axis)
    return 0.5 * (upper - lower)

def neighbours(field, axis):
    size = field.shape[axis]
    widths = [(0, 0)] * field.ndim
    widths[axis] = (1, 1)
    padded = jnp.pad(field, widths)
    return lax.slice_in_dim(padded, 2, size + 2, axis=axis) + lax.slice_in_dim(padded, 0, size, axis=axis)

def kernel_apply(field):
    nsum = neighbours(field, 1) + neighbours(field, 2) + neighbours(field, 3)
    return field + smoothing * (nsum - 6.0 * field)

def transport(template, momentum_one, count):
    velocity = kernel_apply(momentum_one)
    image = template
    for step in range(STEPS):
        active = (step < count).astype(jnp.float32)
        advect = velocity[0] * central(image, 0) + velocity[1] * central(image, 1) + velocity[2] * central(image, 2)
        image = image - time_step * active * advect
    return image

def reference(template, momentum, targets, step_count):

    def per_subject(items):
        moment_one, target_one, count = items
        warped_one, pullback = jax.vjp(lambda tmpl, mom: transport(tmpl, mom, count), template, moment_one)
        grad_tmpl, grad_mom = pullback(warped_one - target_one)
        return (warped_one, grad_tmpl, grad_mom)
    warped, grads_tmpl, grads_mom = lax.map(per_subject, (momentum, targets, step_count))
    return (warped, lax.optimization_barrier(jnp.sum(grads_tmpl, axis=0)), grads_mom)
```

```python
import jax
import jax.numpy as jnp
from jax import lax
from jax.experimental import pallas as pl
from jax.experimental.pallas import tpu as pltpu
from jax.sharding import PartitionSpec as P

time_step = 0.15
smoothing = 0.1
half = 0.5 * time_step
centre = 1.0 - 6.0 * smoothing
f32 = jnp.float32


def load(ref, *at):
    at = at + (slice(None),)
    rows = ref.shape[-2] // 8
    return tuple(ref[at + (pl.ds(128 * h, 128),)].reshape(rows, 8, 128) for h in (0, 1))


def store(ref, plane, *at):
    at = at + (slice(None),)
    for h in (0, 1):
        ref[at + (pl.ds(128 * h, 128),)] = plane[h].reshape(-1, 128)


def load_t(ref, p):
    return tuple(ref[:, p, :, pl.ds(128 * h, 128)] for h in (0, 1))


def each(fn, *planes):
    return tuple(fn(*x) for x in zip(*planes))


def add(*planes):
    total = planes[0]
    for plane in planes[1:]:
        total = each(lambda a, b: a + b, total, plane)
    return total


def sub(a, b):
    return each(lambda x, y: x - y, a, b)


def mul(a, b):
    return each(lambda x, y: x * y, a, b)


def scale(a, factor):
    return each(lambda x: x * factor, a)


def y_sides(x):
    row = lax.broadcasted_iota(jnp.int32, (1, 8, 128), 1)
    down, up = pltpu.roll(x, 1, axis=1), pltpu.roll(x, 7, axis=1)
    none = jnp.zeros((1, 8, 128), f32)
    before = jnp.where(row == 0, jnp.concatenate([none, down[:-1]], axis=0), down)
    after = jnp.where(row == 7, jnp.concatenate([up[1:], none], axis=0), up)
    return before, after


def x_sides(plane):
    lane = lax.broadcasted_iota(jnp.int32, (1, 8, 128), 2)
    right = each(lambda x: pltpu.roll(x, 1, axis=2), plane)
    left = each(lambda x: pltpu.roll(x, 127, axis=2), plane)
    before = (jnp.where(lane == 0, 0.0, right[0]), jnp.where(lane == 0, right[0], right[1]))
    after = (jnp.where(lane == 127, left[1], left[0]), jnp.where(lane == 127, 0.0, left[1]))
    return before, after


def dy(plane):
    def one(x):
        before, after = y_sides(x)
        return after - before

    return each(one, plane)


def dx(plane):
    before, after = x_sides(plane)
    return sub(after, before)


def smooth(mid, inner, outer, a, b):
    def ysum(x):
        before, after = y_sides(x)
        return after + before

    before, after = x_sides(mid)
    total = add(inner, outer, each(ysum, mid), add(before, after))
    return each(lambda m, t: a * m + b * t, mid, total)


def dz(inner, outer, toward):
    return sub(inner, outer) if toward > 0 else sub(outer, inner)


def forward(mid, inner, outer, w, toward=1):
    change = add(mul(w[0], dz(inner, outer, toward)), mul(w[1], dy(mid)), mul(w[2], dx(mid)))
    return sub(mid, change)


def backward(mid, flux_inner, flux_outer, wy, wx, toward=1, active=None):
    change = add(dz(flux_inner, flux_outer, toward), dy(mul(wy, mid)), dx(mul(wx, mid)))
    return add(mid, change if active is None else scale(change, active))


def grads(adj, mid, inner, outer, toward=1):
    return [mul(adj, dz(inner, outer, toward)), mul(adj, dy(mid)), mul(adj, dx(mid))]


def natural(odd, j):
    return j + odd * (7 - 2 * j)


ROLES = (0, 1)
TOWARD = (1, -1)


def t_side(odd, role):
    if role == 0:
        return odd, 1 - odd, 2 + 7 * odd, 2 + odd * 5 + 1
    return 11 - odd, 10 + odd, 9 - 7 * odd, 8 - 5 * odd


def inner_1(info, m, t, w_in, i1_in, i2_in):
    s = pl.program_id(0)
    odd = info[4]
    sign = (1 - 2 * odd).astype(f32)

    def first(j, _):
        w = []
        for c in range(3):
            turn = sign if c == 0 else 1.0
            v = smooth(
                load(m, 0, c, natural(odd, j)),
                load(m, 0, c, natural(odd, j + 1)),
                load(m, 0, c, natural(odd, j - 1)),
                half * centre * turn,
                half * smoothing * turn,
            )
            store(w_in, v, 0, c, j - 1)
            w.append(v)
        at = lambda i: load_t(t, 2 + natural(odd, i))
        store(i1_in, forward(at(j), at(j + 1), at(j - 1), w), 0, j - 1)
        return 0

    lax.fori_loop(1, 7, first, 0)
    active = info[s] > 1

    @pl.when(active)
    def _():
        def second(j, _):
            at = lambda i: load(i1_in, 0, i - 1)
            w = [load(w_in, 0, c, j - 1) for c in range(3)]
            store(i2_in, forward(at(j), at(j + 1), at(j - 1), w), 0, j - 2)
            return 0

        lax.fori_loop(2, 6, second, 0)

    @pl.when(jnp.logical_not(active))
    def _():
        i2_in[...] = i1_in[:, 1:5]


def outer_1(info, *refs):
    ms, mr, t, wp, i1p = refs[0:2], refs[2:4], refs[4], refs[5:7], refs[7:9]
    w_out, i1_out, send = refs[9:11], refs[11:13], refs[13:15]
    s = pl.program_id(0)
    odd = info[4]
    sign = (1 - 2 * odd).astype(f32)
    for r in ROLES:
        to = TOWARD[r]
        p0 = odd if r == 0 else 1 - odd
        p1 = 1 - p0
        h1, h2 = p1, p0
        near = r * 1
        far = 1 - near
        inside = info[5].astype(f32) if r == 0 else 1.0
        ws = [[], []]
        for c in range(3):
            turn = sign if c == 0 else 1.0
            m_h1, m_p0 = load(mr[r], 0, c, h1), load(ms[r], 0, c, p0)
            a, b = half * centre * turn, half * smoothing * turn
            wh = smooth(m_h1, m_p0, load(mr[r], 0, c, h2), a * inside, b * inside)
            w0 = smooth(m_p0, load(ms[r], 0, c, p1), m_h1, a, b)
            store(w_out[r], wh, 0, c, 0)
            store(w_out[r], w0, 0, c, 1)
            ws[0].append(wh)
            ws[1].append(w0)
        th2, th1, tp0, tp1 = (load_t(t, at) for at in t_side(odd, r))
        i_h1 = forward(th1, tp0, th2, ws[0], to)
        i_p0 = forward(tp0, tp1, th1, ws[1], to)
        store(i1_out[r], i_h1, 0, 0)
        store(i1_out[r], i_p0, 0, 1)

        @pl.when(info[s] > 1)
        def _():
            i_p1, i_p2 = load(i1p[r], 0, near), load(i1p[r], 0, far)
            i_h1, i_p0 = load(i1_out[r], 0, 0), load(i1_out[r], 0, 1)
            w0 = [load(w_out[r], 0, c, 1) for c in range(3)]
            w1 = [load(wp[r], 0, c, near) for c in range(3)]
            store(send[r], forward(i_p0, i_p1, i_h1, w0, to), 0, 0)
            store(send[r], forward(i_p1, i_p2, i_p0, w1, to), 0, 1)

        @pl.when(info[s] <= 1)
        def _():
            store(send[r], load(i1_out[r], 0, 1), 0, 0)
            store(send[r], load(i1p[r], 0, near), 0, 1)


def gather_planes(x, sides, inner):
    x[0] = sides[0][0, 0]
    x[1] = sides[0][0, 1]
    x[7] = sides[1][0, 0]
    x[6] = sides[1][0, 1]
    x[2:6] = inner[0]


def inner_2(info, w_in, i2_in, s1z, s1c, targets, i3_in, a4_in, i4_in, x):
    s = pl.program_id(0)
    odd = info[4]
    gather_planes(x, (s1z, s1c), i2_in)

    @pl.when(info[s] > 2)
    def _():
        def step(j, _):
            w = [load(w_in, 0, c, j - 1) for c in range(3)]
            store(i3_in, forward(load(x, j), load(x, j + 1), load(x, j - 1), w), 0, j - 1)
            return 0

        lax.fori_loop(1, 7, step, 0)

    @pl.when(info[s] <= 2)
    def _():
        i3_in[0] = x[1:7]

    @pl.when(info[s] > 3)
    def _():
        def step(j, _):
            at = lambda i: load(i3_in, 0, i - 1)
            w = [load(w_in, 0, c, j - 1) for c in range(3)]
            image = forward(at(j), at(j + 1), at(j - 1), w)
            store(i4_in, image, 0, j - 2)
            store(a4_in, sub(image, load(targets, 0, natural(odd, j))), 0, j - 2)
            return 0

        lax.fori_loop(2, 6, step, 0)

    @pl.when(info[s] <= 3)
    def _():
        def step(j, _):
            image = load(i3_in, 0, j - 1)
            store(i4_in, image, 0, j - 2)
            store(a4_in, sub(image, load(targets, 0, natural(odd, j))), 0, j - 2)
            return 0

        lax.fori_loop(2, 6, step, 0)


def outer_2(info, *refs):
    r1, wb, wp, s1, i2p, i3p, tg = (refs[2 * i : 2 * i + 2] for i in range(7))
    i3_out, i4_out, a4_out, send = (refs[14 + 2 * i : 16 + 2 * i] for i in range(4))
    s = pl.program_id(0)
    odd = info[4]
    for r in ROLES:
        to, near, far = TOWARD[r], r, 1 - r
        p0 = odd if r == 0 else 1 - odd

        @pl.when(info[s] > 2)
        def _():
            i_h1, i_h2 = load(r1[r], 0, 0), load(r1[r], 0, 1)
            i_p0, i_p1 = load(s1[r], 0, 0), load(s1[r], 0, 1)
            wh = [load(wb[r], 0, c, 0) for c in range(3)]
            w0 = [load(wb[r], 0, c, 1) for c in range(3)]
            store(i3_out[r], forward(i_h1, i_p0, i_h2, wh, to), 0, 0)
            store(i3_out[r], forward(i_p0, i_p1, i_h1, w0, to), 0, 1)

        @pl.when(info[s] <= 2)
        def _():
            i3_out[r][0, 0] = r1[r][0, 0]
            i3_out[r][0, 1] = s1[r][0, 0]

        @pl.when(info[s] > 3)
        def _():
            i_h1, i_p0 = load(i3_out[r], 0, 0), load(i3_out[r], 0, 1)
            i_p1, i_p2 = load(i3p[r], 0, near), load(i3p[r], 0, far)
            w0 = [load(wb[r], 0, c, 1) for c in range(3)]
            w1 = [load(wp[r], 0, c, near) for c in range(3)]
            store(i4_out[r], forward(i_p0, i_p1, i_h1, w0, to), 0, 0)
            store(i4_out[r], forward(i_p1, i_p2, i_p0, w1, to), 0, 1)

        @pl.when(info[s] <= 3)
        def _():
            i4_out[r][0, 0] = i3_out[r][0, 1]
            i4_out[r][0, 1] = i3p[r][0, near]

        store(send[r], sub(load(i4_out[r], 0, 0), load(tg[r], 0, p0)), 0, 0)
        a_p1 = sub(load(i4_out[r], 0, 1), load(tg[r], 0, 1 - p0))
        store(a4_out[r], a_p1, 0, 0)
        store(send[r], mul(load(wp[r], 0, 0, near), a_p1), 0, 1)


def inner_3(info, *refs):
    w_in, wbz, wbc, s2z, s2c, a4z, a4c, a4_in, i3_in, i3z, i3c, i2_in, s1z, s1c, i1_in, i4_in, i4z, i4c = refs[:18]
    a3_in, a2_in, g_in, warped, a, f, x = refs[18:]
    s = pl.program_id(0)
    odd = info[4]
    a[0], a[7] = s2z[0, 0], s2c[0, 0]
    a[1], a[6] = a4z[0, 0], a4c[0, 0]
    a[2:6] = a4_in[0]
    for r, side in ((0, i4z), (1, i4c)):
        p0, p1 = (0, 1) if r == 0 else (7, 6)
        warped[0, natural(odd, p0)] = side[0, 0]
        warped[0, natural(odd, p1)] = side[0, 1]

    def copy(j, _):
        warped[0, natural(odd, j)] = i4_in[0, j - 2]
        return 0

    lax.fori_loop(2, 6, copy, 0)

    @pl.when(info[s] > 3)
    def _():
        x[0], x[7] = i3z[0, 0], i3c[0, 0]
        x[1:7] = i3_in[0]
        f[0] = wbz[0, 0, 0] * a[0]
        f[7] = wbc[0, 0, 0] * a[7]
        f[1:7] = w_in[0, 0] * a[1:7]

        def step(j, _):
            mid = load(a, j)
            wy, wx = (load(w_in, 0, c, j - 1) for c in (1, 2))
            store(a3_in, backward(mid, load(f, j + 1), load(f, j - 1), wy, wx), 0, j - 1)
            for c, g in enumerate(grads(mid, load(x, j), load(x, j + 1), load(x, j - 1))):
                store(g_in, g, 0, c, j - 1)
            return 0

        lax.fori_loop(1, 7, step, 0)

    @pl.when(info[s] <= 3)
    def _():
        a3_in[0] = a[1:7]
        g_in[...] = jnp.zeros(g_in.shape, f32)

    @pl.when(info[s] > 2)
    def _():
        gather_planes(x, (s1z, s1c), i2_in)
        f[1:7] = w_in[0, 0] * a3_in[0]

        def gradient(j):
            adj = load(a3_in, 0, j - 1)
            for c, g in enumerate(grads(adj, load(x, j), load(x, j + 1), load(x, j - 1))):
                store(g_in, add(load(g_in, 0, c, j - 1), g), 0, c, j - 1)
            return adj

        gradient(1)
        gradient(6)

        def step(j, _):
            mid = gradient(j)
            wy, wx = (load(w_in, 0, c, j - 1) for c in (1, 2))
            store(a2_in, backward(mid, load(f, j + 1), load(f, j - 1), wy, wx), 0, j - 2)
            return 0

        lax.fori_loop(2, 6, step, 0)

    @pl.when(info[s] <= 2)
    def _():
        a2_in[0] = a3_in[0, 1:5]

    @pl.when(info[s] > 1)
    def _():
        def step(j, _):
            at = lambda i: load(i1_in, 0, i - 1)
            for c, g in enumerate(grads(load(a2_in, 0, j - 2), at(j), at(j + 1), at(j - 1))):
                store(g_in, add(load(g_in, 0, c, j - 1), g), 0, c, j - 1)
            return 0

        lax.fori_loop(2, 6, step, 0)


def outer_3(info, *refs):
    r2, wb, wp, s2, a3p, i3b, i3p, r1, s1, i1b, i1p = (refs[2 * i : 2 * i + 2] for i in range(11))
    a2_out, g_out, send, a3 = (refs[22 + 2 * i : 24 + 2 * i] for i in range(4))
    s = pl.program_id(0)
    for r in ROLES:
        to, near, far = TOWARD[r], r, 1 - r
        g = g_out[r]

        @pl.when(info[s] > 3)
        def _():
            a_h1, a_p0 = load(r2[r], 0, 0), load(s2[r], 0, 0)
            f_h2, f_p1 = scale(load(r2[r], 0, 1), -1.0), load(s2[r], 0, 1)
            wh = [load(wb[r], 0, c, 0) for c in range(3)]
            w0 = [load(wb[r], 0, c, 1) for c in range(3)]
            store(a3[r], backward(a_h1, mul(w0[0], a_p0), f_h2, wh[1], wh[2], to), 0)
            store(a3[r], backward(a_p0, f_p1, mul(wh[0], a_h1), w0[1], w0[2], to), 1)
            i_h1, i_p0, i_p1 = load(i3b[r], 0, 0), load(i3b[r], 0, 1), load(i3p[r], 0, near)
            store(g, mul(a_h1, dy(i_h1)), 0, 1, 0)
            store(g, mul(a_h1, dx(i_h1)), 0, 2, 0)
            for c, value in enumerate(grads(a_p0, i_p0, i_p1, i_h1, to)):
                store(g, value, 0, c, 1)

        @pl.when(info[s] <= 3)
        def _():
            a3[r][0] = r2[r][0, 0]
            a3[r][1] = s2[r][0, 0]
            g[...] = jnp.zeros(g.shape, f32)

        @pl.when(info[s] > 2)
        def _():
            a_h1, a_p0 = load(a3[r], 0), load(a3[r], 1)
            a_p1, a_p2 = load(a3p[r], 0, near), load(a3p[r], 0, far)
            wh0 = load(wb[r], 0, 0, 0)
            w0 = [load(wb[r], 0, c, 1) for c in range(3)]
            w1 = [load(wp[r], 0, c, near) for c in range(3)]
            store(a2_out[r], backward(a_p0, mul(w1[0], a_p1), mul(wh0, a_h1), w0[1], w0[2], to), 0, 0)
            f_p2 = mul(load(wp[r], 0, 0, far), a_p2)
            store(a2_out[r], backward(a_p1, f_p2, mul(w0[0], a_p0), w1[1], w1[2], to), 0, 1)
            i_h1, i_p0, i_p1 = load(r1[r], 0, 0), load(s1[r], 0, 0), load(s1[r], 0, 1)
            store(g, add(load(g, 0, 1, 0), mul(a_h1, dy(i_h1))), 0, 1, 0)
            store(g, add(load(g, 0, 2, 0), mul(a_h1, dx(i_h1))), 0, 2, 0)
            for c, value in enumerate(grads(a_p0, i_p0, i_p1, i_h1, to)):
                store(g, add(load(g, 0, c, 1), value), 0, c, 1)

        @pl.when(info[s] <= 2)
        def _():
            a2_out[r][0, 0] = a3[r][1]
            a2_out[r][0, 1] = a3p[r][0, near]

        @pl.when(info[s] > 1)
        def _():
            i_h1, i_p0 = load(i1b[r], 0, 0), load(i1b[r], 0, 1)
            i_p1, i_p2 = load(i1p[r], 0, near), load(i1p[r], 0, far)
            for c, value in enumerate(grads(load(a2_out[r], 0, 0), i_p0, i_p1, i_h1, to)):
                store(g, add(load(g, 0, c, 1), value), 0, c, 1)
            for c, value in enumerate(grads(load(a2_out[r], 0, 1), i_p1, i_p2, i_p0, to)):
                store(g, value, 0, c, 2)

        @pl.when(info[s] <= 1)
        def _():
            g[0, :, 2] = jnp.zeros(g.shape[1:2] + g.shape[3:], f32)

        send[r][0, 0] = a2_out[r][0, 0]
        send[r][0, 1] = wp[r][0, 0, near] * a2_out[r][0, 1]
        send[r][0, 2] = g[0, 0, 1]


def final(mid, inner, outer, turn):
    return smooth(mid, inner, outer, -half * centre * turn, -half * smoothing * turn)


def inner_4(info, *refs):
    w_in, wbz, wbc, a2_in, a2z, a2c, t, g_in, gz, gc = refs[:10]
    a1_in, g_full, total, mg, a, f = refs[10:]
    s = pl.program_id(0)
    odd = info[4]
    sign = (1 - 2 * odd).astype(f32)
    gather_planes(a, (a2z, a2c), a2_in)
    f[0] = wbz[0, 0, 0] * a[0]
    f[7] = wbc[0, 0, 0] * a[7]
    f[1:7] = w_in[0, 0] * a[1:7]
    @pl.when(s == 0)
    def _():
        total[...] = jnp.zeros(total.shape, f32)

    def gradient(j, adj):
        at = lambda i: load_t(t, 2 + natural(odd, i))
        for c, g in enumerate(grads(adj, at(j), at(j + 1), at(j - 1))):
            store(g_full, add(load(g_in, 0, c, j - 1), g), 0, c, j - 1)

    @pl.when(info[s] > 1)
    def _():
        def step(j, _):
            mid = load(a, j)
            wy, wx = (load(w_in, 0, c, j - 1) for c in (1, 2))
            adj = backward(mid, load(f, j + 1), load(f, j - 1), wy, wx)
            store(a1_in, adj, 0, j - 1)
            gradient(j, adj)
            return 0

        lax.fori_loop(1, 7, step, 0)

    @pl.when(info[s] <= 1)
    def _():
        def step(j, _):
            adj = load(a, j)
            store(a1_in, adj, 0, j - 1)
            gradient(j, adj)
            return 0

        lax.fori_loop(1, 7, step, 0)

    g_full[0, :, 0] += gz[0, :, 0]
    g_full[0, :, 5] += gc[0, :, 0]
    f[1:7] = w_in[0, 0] * a1_in[0]

    def last(j, _):
        mid = load(a1_in, 0, j - 1)
        wy, wx = (load(w_in, 0, c, j - 1) for c in (1, 2))
        adj = backward(mid, load(f, j + 1), load(f, j - 1), wy, wx)
        for h in (0, 1):
            total[:, j - 2, :, pl.ds(128 * h, 128)] += adj[h]
        for c in range(3):
            at = lambda i: load(g_full, 0, c, i - 1)
            store(mg, final(at(j), at(j + 1), at(j - 1), sign if c == 0 else 1.0), 0, c, natural(odd, j))
        return 0

    lax.fori_loop(2, 6, last, 0)


def outer_4(info, *refs):
    r3, wb, wp, s3, a1p, gb, gp, i1b = (refs[2 * i : 2 * i + 2] for i in range(8))
    t, total_in, mg_in = refs[16:19]
    total, mg, made, sems = refs[19:]
    s = pl.program_id(0)
    odd = info[4]
    sign = (1 - 2 * odd).astype(f32)
    slot = lax.rem(s, 2)

    def copies(which, at):
        z_first, c_first = 6 * odd, 6 - 6 * odd
        return [
            pltpu.make_async_copy(made.at[which, r], mg.at[at, :, pl.ds(first, 2)], sems.at[which, r])
            for r, first in ((0, z_first), (1, c_first))
        ]

    @pl.when(s == 0)
    def _():
        total[...] = jnp.zeros(total.shape, f32)

        def copy(j, _):
            total[:, natural(odd, j)] = total_in[:, j - 2]
            return 0

        lax.fori_loop(2, 6, copy, 0)

    @pl.when(s >= 2)
    def _():
        for copy in copies(slot, s - 2):
            copy.wait()

    for r in ROLES:
        to, near, far = TOWARD[r], r, 1 - r
        p0 = odd if r == 0 else 1 - odd
        n0, n1 = (natural(odd, 0), natural(odd, 1)) if r == 0 else (natural(odd, 7), natural(odd, 6))
        inside = info[5].astype(f32) if r == 0 else 1.0
        a_h1, a_p0 = load(r3[r], 0, 0), load(s3[r], 0, 0)
        f_h2, f_p1 = scale(load(r3[r], 0, 1), -1.0), load(s3[r], 0, 1)
        wh = [load(wb[r], 0, c, 0) for c in range(3)]
        w0 = [load(wb[r], 0, c, 1) for c in range(3)]
        w1 = [load(wp[r], 0, c, near) for c in range(3)]
        step_one = (info[s] > 1).astype(f32)
        b_h1 = backward(a_h1, mul(w0[0], a_p0), f_h2, wh[1], wh[2], to, step_one)
        b_p0 = backward(a_p0, f_p1, mul(wh[0], a_h1), w0[1], w0[2], to, step_one)
        b_p1, b_p2 = load(a1p[r], 0, near), load(a1p[r], 0, far)
        c_p0 = backward(b_p0, mul(w1[0], b_p1), mul(wh[0], b_h1), w0[1], w0[2], to)
        c_p1 = backward(b_p1, mul(load(wp[r], 0, 0, far), b_p2), mul(w0[0], b_p0), w1[1], w1[2], to)
        for n, value in ((n0, c_p0), (n1, c_p1)):
            for h in (0, 1):
                total[:, n, :, pl.ds(128 * h, 128)] += value[h]
        th2, th1, tp0, tp1 = (load_t(t, at) for at in t_side(odd, r))
        i_h1 = load(i1b[r], 0, 0)
        a_one = scale(a_h1, step_one)
        g_h1 = [
            add(scale(load(r3[r], 0, 2), -1.0), mul(b_h1, dz(tp0, th2, to))),
            add(load(gb[r], 0, 1, 0), mul(a_one, dy(i_h1)), mul(b_h1, dy(th1))),
            add(load(gb[r], 0, 2, 0), mul(a_one, dx(i_h1)), mul(b_h1, dx(th1))),
        ]
        g_p0 = grads(b_p0, tp0, tp1, th1, to)
        for c in range(3):
            turn = sign if c == 0 else 1.0
            g0 = add(load(gb[r], 0, c, 1), g_p0[c])
            g1, g2 = load(gp[r], 0, c, near), load(gp[r], 0, c, far)
            store(made, final(g0, g1, scale(g_h1[c], inside), turn), slot, r, c, p0)
            store(made, final(g1, g2, g0, turn), slot, r, c, 1 - p0)

    for copy in copies(slot, s):
        copy.start()

    @pl.when(s == 3)
    def _():
        for copy in copies(1 - slot, s - 1) + copies(slot, s):
            copy.wait()


ROWS, COLS = 64, 256
PLANE = (ROWS, COLS)


def planes(count, at=0):
    return pl.BlockSpec((1, count) + PLANE, lambda s, info: (s, at, 0, 0))


def vec(count, at=0):
    return pl.BlockSpec((1, 3, count) + PLANE, lambda s, info: (s, 0, at, 0, 0))


def vec_z(at):
    return pl.BlockSpec((1, 1, 1) + PLANE, lambda s, info: (s, 0, at, 0, 0))


def whole(shape):
    return pl.BlockSpec(shape, lambda s, info: (0,) * len(shape))


def call(kernel, info, ins, outs, scratch=(), alias={}, work=1.0, name=None):
    arrays, in_specs = zip(*ins)
    shapes, out_specs = zip(*outs)
    moved = 4 * sum(a.size for a in arrays) // 2
    return pl.pallas_call(
        kernel,
        grid_spec=pltpu.PrefetchScalarGridSpec(
            num_scalar_prefetch=1,
            grid=(4,),
            in_specs=list(in_specs),
            out_specs=list(out_specs),
            scratch_shapes=list(scratch),
        ),
        out_shape=[jax.ShapeDtypeStruct(shape, f32) for shape in shapes],
        input_output_aliases=alias,
        compiler_params=pltpu.CompilerParams(vmem_limit_bytes=32 * 1024 * 1024),
        cost_estimate=pl.CostEstimate(flops=int(work * 1e7), bytes_accessed=moved, transcendentals=0),
        name=name,
    )(info, *arrays)


def shards(template, momentum, targets, step_count):
    count = lax.axis_size("space")
    groups = lax.axis_size("subj")
    place = lax.axis_index("space")
    odd = place % 2
    core_pairs = [(i, i ^ 1) for i in range(count)]
    chip_pairs = [(i, ((i + 1) ^ 1) - 1) for i in range(1, count - 1)]

    def swap(pair):
        return lax.ppermute(pair[0], "space", chip_pairs), lax.ppermute(pair[1], "space", core_pairs)

    inside = jnp.logical_and(place > 0, place < count - 1).astype(jnp.int32)
    info = jnp.concatenate([step_count, jnp.stack([odd, inside]).astype(jnp.int32)])

    def ends(array, dim):
        return tuple(lax.dynamic_slice_in_dim(array, at, 2, dim) for at in (6 * odd, 6 - 6 * odd))

    subjects = step_count.shape[0]

    def shape(*lead):
        return (subjects,) + lead + PLANE

    t_halo = swap(ends(template, 0))
    ms = ends(momentum, 2)
    mr = swap(ms)
    wide = jnp.concatenate([t_halo[0], template, t_halo[1]], axis=0)
    t = lax.all_to_all(jnp.broadcast_to(wide[None], (groups,) + wide.shape), "subj", 0, 0)
    t_spec = (t, whole(t.shape))

    def both(pair, *specs):
        return [(pair[0], specs[0]), (pair[1], specs[-1])]

    w_in, i1_in, i2_in = call(
        inner_1,
        info,
        [(momentum, vec(8)), t_spec],
        [(shape(3, 6), vec(6)), (shape(6), planes(6)), (shape(4), planes(4))],
        name="inner_1",
    )
    wp = both((w_in, w_in), vec(2, 0), vec(2, 2))
    i1p = both((i1_in, i1_in), planes(2, 0), planes(2, 2))
    two = [(shape(2), planes(2))] * 2
    three = [(shape(3), planes(3))] * 2
    *rest, s1z, s1c = call(
        outer_1,
        info,
        both(ms, vec(2)) + both(mr, vec(2)) + [t_spec] + wp + i1p,
        [(shape(3, 2), vec(2))] * 2 + two + two,
        name="outer_1",
    )
    wb, i1b, s1 = rest[0:2], rest[2:4], (s1z, s1c)

    r1 = swap(s1)
    i3_in, a4_in, i4_in = call(
        inner_2,
        info,
        [(w_in, vec(6)), (i2_in, planes(4))] + both(s1, planes(2)) + [(targets, planes(8))],
        [(shape(6), planes(6)), (shape(4), planes(4)), (shape(4), planes(4))],
        [pltpu.VMEM((8,) + PLANE, f32)],
        name="inner_2",
    )
    i3p = both((i3_in, i3_in), planes(2, 0), planes(2, 2))
    z_end = pl.BlockSpec((1, 2) + PLANE, lambda s, info: (s, 3 * info[4], 0, 0))
    c_end = pl.BlockSpec((1, 2) + PLANE, lambda s, info: (s, 3 - 3 * info[4], 0, 0))
    out = call(
        outer_2,
        info,
        both(r1, planes(2))
        + both(wb, vec(2))
        + wp
        + both(s1, planes(2))
        + both((i2_in, i2_in), planes(1, 0), planes(1, 3))
        + i3p
        + both((targets, targets), z_end, c_end),
        two + two + [(shape(1), planes(1))] * 2 + two,
        name="outer_2",
    )
    i3b, i4b, a4b, s2 = (out[2 * i : 2 * i + 2] for i in range(4))

    r2 = swap(s2)
    wb_z = both(wb, vec_z(1))
    a3_in, a2_in, g_in, warped = call(
        inner_3,
        info,
        [(w_in, vec(6))]
        + wb_z
        + both(s2, planes(1))
        + both(a4b, planes(1))
        + [(a4_in, planes(4)), (i3_in, planes(6))]
        + both(i3b, planes(1, 1))
        + [(i2_in, planes(4))]
        + both(s1, planes(2))
        + [(i1_in, planes(6)), (i4_in, planes(4))]
        + both(i4b, planes(2)),
        [(shape(6), planes(6)), (shape(4), planes(4)), (shape(3, 6), vec(6)), (shape(8), planes(8))],
        [pltpu.VMEM((8,) + PLANE, f32)] * 3,
        name="inner_3",
    )
    out = call(
        outer_3,
        info,
        both(r2, planes(2))
        + both(wb, vec(2))
        + wp
        + both(s2, planes(2))
        + both((a3_in, a3_in), planes(2, 0), planes(2, 2))
        + both(i3b, planes(2))
        + i3p
        + both(r1, planes(2))
        + both(s1, planes(2))
        + both(i1b, planes(2))
        + i1p,
        two + [(shape(3, 3), vec(3))] * 2 + three,
        [pltpu.VMEM((2,) + PLANE, f32)] * 2,
        name="outer_3",
    )
    a2b, gb, s3 = (out[2 * i : 2 * i + 2] for i in range(3))

    r3 = swap(s3)
    tile = (groups, 8, 8, COLS)
    small = (groups, 4, 8, COLS)
    a1_in, g_full, total, mg = call(
        inner_4,
        info,
        [(w_in, vec(6))]
        + wb_z
        + [(a2_in, planes(4))]
        + both(a2b, planes(2))
        + [t_spec, (g_in, vec(6))]
        + both(gb, vec(1, 2)),
        [(shape(6), planes(6)), (shape(3, 6), vec(6)), (small, whole(small)), (shape(3, 8), vec(8))],
        [pltpu.VMEM((8,) + PLANE, f32)] * 2,
        name="inner_4",
    )
    anywhere = pl.BlockSpec(memory_space=pl.ANY)
    total, momentum_gradient = call(
        outer_4,
        info,
        both(r3, planes(3))
        + both(wb, vec(2))
        + wp
        + both(s3, planes(3))
        + both((a1_in, a1_in), planes(2, 0), planes(2, 2))
        + both(gb, vec(3))
        + both((g_full, g_full), vec(2, 0), vec(2, 2))
        + both(i1b, planes(2))
        + [t_spec, (total, whole(small)), (mg, anywhere)],
        [(tile, whole(tile)), (shape(3, 8), anywhere)],
        [pltpu.VMEM((2, 2, 3, 2) + PLANE, f32), pltpu.SemaphoreType.DMA((2, 2))],
        alias={19: 1},
        name="outer_4",
    )
    parts = lax.all_to_all(total, "subj", 0, 0)
    template_gradient = jnp.sum(parts, axis=0)
    return (warped, template_gradient, momentum_gradient)


def solution(mesh):
    in_specs = (
        P("space", "subj", None),
        P("subj", None, "space", None, None),
        P("subj", "space", None, None),
        P("subj"),
    )
    out_specs = (
        P("subj", "space", None, None),
        P("space", "subj", None),
        P("subj", None, "space", None, None),
    )
    return jax.shard_map(shards, mesh=mesh, in_specs=in_specs, out_specs=out_specs, check_vma=False)
```

```python
import jax
import jax.numpy as jnp
from jax import lax
from jax.experimental import pallas as pl
from jax.experimental.pallas import tpu as pltpu
from jax.sharding import PartitionSpec as P

time_step = 0.15
smoothing = 0.1
half = 0.5 * time_step
centre = 1.0 - 6.0 * smoothing
f32 = jnp.float32


class Plane:
    def __init__(self, rows):
        self.rows, self.known, self.rolled = rows, {}, {}

    def at(self, b):
        if b not in self.known:
            self.known[b] = tuple(self.rows(b))
        return self.known[b]

    def turned(self, b, by):
        if (b, by) not in self.rolled:
            self.rolled[b, by] = tuple(pltpu.roll(x, by, axis=0) for x in self.at(b))
        return self.rolled[b, by]


BLOCKS = 8


def halves(h):
    return pl.ds(128 * h, 128)


def load(ref, *at):
    return Plane(lambda b: [ref[at + (pl.ds(8 * b, 8), halves(h))] for h in (0, 1)])


def store(ref, plane, *at):
    store_all([(ref, plane, at)])


def store_all(targets):
    for b in range(BLOCKS):
        for ref, plane, at in targets:
            for h, value in enumerate(plane.at(b)):
                ref[at + (pl.ds(8 * b, 8), halves(h))] = value


def add_t(ref, plane, p):
    for b in range(BLOCKS):
        for h, value in enumerate(plane.at(b)):
            ref[b, p, :, halves(h)] += value


def each(fn, *planes):
    return Plane(lambda b: [fn(*x) for x in zip(*(plane.at(b) for plane in planes))])


def add(*planes):
    total = planes[0]
    for plane in planes[1:]:
        total = each(lambda a, b: a + b, total, plane)
    return total


def sub(a, b):
    return each(lambda x, y: x - y, a, b)


def mul(a, b):
    return each(lambda x, y: x * y, a, b)


def scale(a, factor):
    return each(lambda x: x * factor, a)


def y_sides(plane):
    def rows(b, by, edge, step):
        row = lax.broadcasted_iota(jnp.int32, (8, 128), 0)
        here, there = plane.turned(b, by), b + step
        over = plane.turned(there, by) if 0 <= there < BLOCKS else (0.0, 0.0)
        return [jnp.where(row == edge, o, x) for o, x in zip(over, here)]

    return Plane(lambda b: rows(b, 1, 0, -1)), Plane(lambda b: rows(b, 7, 7, 1))


def x_sides(plane):
    def before(b):
        lane = lax.broadcasted_iota(jnp.int32, (8, 128), 1)
        left, right = (pltpu.roll(x, 1, axis=1) for x in plane.at(b))
        return jnp.where(lane == 0, 0.0, left), jnp.where(lane == 0, left, right)

    def after(b):
        lane = lax.broadcasted_iota(jnp.int32, (8, 128), 1)
        left, right = (pltpu.roll(x, 127, axis=1) for x in plane.at(b))
        return jnp.where(lane == 127, right, left), jnp.where(lane == 127, 0.0, right)

    return Plane(before), Plane(after)


def dy(plane):
    before, after = y_sides(plane)
    return sub(after, before)


def dx(plane):
    before, after = x_sides(plane)
    return sub(after, before)


def smooth(mid, inner, outer, a, b):
    total = add(*(plane for plane in (inner, outer) if plane is not None), *y_sides(mid), *x_sides(mid))
    return each(lambda m, t: a * m + b * t, mid, total)


def dz(inner, outer, toward):
    return sub(inner, outer) if toward > 0 else sub(outer, inner)


def forward(mid, inner, outer, w, toward=1):
    change = add(mul(w[0], dz(inner, outer, toward)), mul(w[1], dy(mid)), mul(w[2], dx(mid)))
    return sub(mid, change)


def forward_by(mid, inner, outer, slopes, w, toward=1):
    change = add(mul(w[0], dz(inner, outer, toward)), mul(w[1], slopes[0]), mul(w[2], slopes[1]))
    return sub(mid, change)


def backward(mid, flux_inner, flux_outer, wy, wx, toward=1, active=None):
    change = add(dz(flux_inner, flux_outer, toward), dy(mul(wy, mid)), dx(mul(wx, mid)))
    return add(mid, change if active is None else scale(change, active))


def grads(adj, mid, inner, outer, toward=1, slopes=None):
    sy, sx = slopes or (dy(mid), dx(mid))
    return [mul(adj, dz(inner, outer, toward)), mul(adj, sy), mul(adj, sx)]


def natural(odd, j):
    return j + odd * (7 - 2 * j)


def unrolled(low, high, step):
    for j in range(low, high):
        step(j, 0)


ROLES = (0, 1)
TOWARD = (1, -1)


def t_load(t, k, role=0):
    return load(t, 2 + k if role == 0 else 9 - k)


def t_slopes(dt, k, role=0):
    return [load(dt, c, 1 + k if role == 0 else 8 - k) for c in (0, 1)]


def template_planes(info, s, *refs):
    *sources, t, dt = refs
    odd, me = info[4], info[6]

    @pl.when(s == 0)
    def _():
        for j in range(-2, 10):
            at = 2 + natural(odd, j)
            if j < 0:
                at = 1 - odd if j == -1 else odd
            if j > 7:
                at = 10 + odd if j == 8 else 11 - odd
            for i, source in enumerate(sources):
                for x in (0, 1):
                    row = pl.multiple_of(8 * jnp.bitwise_xor(me, 2 * i + x), 8)
                    t[j + 2, pl.ds(row, 8)] = source[x, at]
        for j in range(-1, 9):
            mid = load(t, j + 2)
            store_all([(dt, dy(mid), (0, j + 1)), (dt, dx(mid), (1, j + 1))])


def velocity_inner(info, s, m, w_in, w_edge, m_edge):
    odd = info[4]
    sign = (1 - 2 * odd).astype(f32)
    for j in range(8):
        for c in range(3):
            turn = sign if c == 0 else 1.0
            v = smooth(
                load(m, 0, c, natural(odd, j)),
                load(m, 0, c, natural(odd, j + 1)) if j < 7 else None,
                load(m, 0, c, natural(odd, j - 1)) if j > 0 else None,
                half * centre * turn,
                half * smoothing * turn,
            )
            if 0 < j < 7:
                store(w_in, v, 0, c, j - 1)
            else:
                store(w_edge, v, 0, c, j // 7)
                m_edge[0, c, j // 7] = m[0, c, natural(odd, j)]


def inner_1(info, s, w_in, t, dt, i1_in, i2_in):
    def first(j, _):
        w = [load(w_in, 0, c, j - 1) for c in range(3)]
        image = forward_by(t_load(t, j), t_load(t, j + 1), t_load(t, j - 1), t_slopes(dt, j), w)
        store(i1_in, image, 0, j - 1)
        return 0

    unrolled(1, 7, first)

    @pl.when(info[s] > 1)
    def _():
        def second(j, _):
            at = lambda i: load(i1_in, 0, i - 1)
            w = [load(w_in, 0, c, j - 1) for c in range(3)]
            store(i2_in, forward(at(j), at(j + 1), at(j - 1), w), 0, j - 2)
            return 0

        unrolled(2, 6, second)

    @pl.when(info[s] <= 1)
    def _():
        i2_in[0] = i1_in[0, 1:5]


def outer_1(info, s, *refs):
    mr, m_edge, w_edge, t, dt, wp, i1p = refs[0:2], *refs[2:6], refs[6:8], refs[8:10]
    w_out, i1_out, send = refs[10:12], refs[12:14], refs[14:16]
    odd = info[4]
    sign = (1 - 2 * odd).astype(f32)
    for r in ROLES:
        to = TOWARD[r]
        h1 = 1 - odd if r == 0 else odd
        inside = info[5].astype(f32) if r == 0 else 1.0
        wh, w0 = [], []
        for c in range(3):
            turn = sign if c == 0 else 1.0
            m_h1, m_p0 = load(mr[r], 0, c, h1), load(m_edge, 0, c, r)
            a, b = half * centre * turn, half * smoothing * turn
            wh.append(smooth(m_h1, m_p0, load(mr[r], 0, c, 1 - h1), a * inside, b * inside))
            w0.append(add(load(w_edge, 0, c, r), scale(m_h1, b)))
        at = lambda k: t_load(t, k, r)
        i_h1 = forward_by(at(-1), at(0), at(-2), t_slopes(dt, -1, r), wh, to)
        i_p0 = forward_by(at(0), at(1), at(-1), t_slopes(dt, 0, r), w0, to)
        targets = [(i1_out[r], i_h1, (0, 0)), (i1_out[r], i_p0, (0, 1))]
        targets += [(w_out[r], w[c], (0, c, i)) for i, w in enumerate((wh, w0)) for c in range(3)]
        store_all(targets)

    @pl.when(info[s] > 1)
    def _():
        for r in ROLES:
            to, near, far = TOWARD[r], r, 1 - r
            i_h1, i_p0 = load(i1_out[r], 0, 0), load(i1_out[r], 0, 1)
            i_p1, i_p2 = load(i1p[r], 0, near), load(i1p[r], 0, far)
            w0 = [load(w_out[r], 0, c, 1) for c in range(3)]
            w1 = [load(wp[r], 0, c, near) for c in range(3)]
            store(send[r], forward(i_p0, i_p1, i_h1, w0, to), 0, 0)
            store(send[r], forward(i_p1, i_p2, i_p0, w1, to), 0, 1)

    @pl.when(info[s] <= 1)
    def _():
        for r in ROLES:
            send[r][0, 0] = i1_out[r][0, 1]
            send[r][0, 1] = i1p[r][0, r]


def gather_planes(x, sides, inner):
    x[0] = sides[0][0, 0]
    x[1] = sides[0][0, 1]
    x[7] = sides[1][0, 0]
    x[6] = sides[1][0, 1]
    x[2:6] = inner[0]


def inner_2(info, s, w_in, i2_in, s1z, s1c, targets, i3_in, i4_in, a4_in, x):
    odd = info[4]
    gather_planes(x, (s1z, s1c), i2_in)

    @pl.when(info[s] > 2)
    def _():
        def step(j, _):
            w = [load(w_in, 0, c, j - 1) for c in range(3)]
            store(i3_in, forward(load(x, j), load(x, j + 1), load(x, j - 1), w), 0, j - 1)
            return 0

        unrolled(1, 7, step)

    @pl.when(info[s] <= 2)
    def _():
        i3_in[0] = x[1:7]

    @pl.when(info[s] > 3)
    def _():
        def step(j, _):
            at = lambda i: load(i3_in, 0, i - 1)
            w = [load(w_in, 0, c, j - 1) for c in range(3)]
            image = forward(at(j), at(j + 1), at(j - 1), w)
            late = sub(image, load(targets, 0, natural(odd, j)))
            store_all([(i4_in, image, (0, j - 2)), (a4_in, late, (0, j - 2))])
            return 0

        unrolled(2, 6, step)

    @pl.when(info[s] <= 3)
    def _():
        def step(j, _):
            image = load(i3_in, 0, j - 1)
            late = sub(image, load(targets, 0, natural(odd, j)))
            store_all([(i4_in, image, (0, j - 2)), (a4_in, late, (0, j - 2))])
            return 0

        unrolled(2, 6, step)


def outer_2(info, s, *refs):
    r1, wb, wp, s1, i3p = (refs[2 * i : 2 * i + 2] for i in range(5))
    targets = refs[10]
    i3_out, i4_out, a4_out, send = (refs[11 + 2 * i : 13 + 2 * i] for i in range(4))
    odd = info[4]

    @pl.when(info[s] > 2)
    def _():
        for r in ROLES:
            i_h1, i_h2 = load(r1[r], 0, 0), load(r1[r], 0, 1)
            i_p0, i_p1 = load(s1[r], 0, 0), load(s1[r], 0, 1)
            wh = [load(wb[r], 0, c, 0) for c in range(3)]
            w0 = [load(wb[r], 0, c, 1) for c in range(3)]
            store(i3_out[r], forward(i_h1, i_p0, i_h2, wh, TOWARD[r]), 0, 0)
            store(i3_out[r], forward(i_p0, i_p1, i_h1, w0, TOWARD[r]), 0, 1)

    @pl.when(info[s] <= 2)
    def _():
        for r in ROLES:
            i3_out[r][0, 0] = r1[r][0, 0]
            i3_out[r][0, 1] = s1[r][0, 0]

    def late(r, i4_p0, i4_p1):
        n = [natural(odd, k if r == 0 else 7 - k) for k in (0, 1)]
        a_p0, a_p1 = sub(i4_p0, load(targets, 0, n[0])), sub(i4_p1, load(targets, 0, n[1]))
        store_all([(i4_out[r], i4_p0, (0, 0)), (send[r], a_p0, (0, 0))])
        f_p1 = mul(load(wp[r], 0, 0, r), a_p1)
        store_all([(i4_out[r], i4_p1, (0, 1)), (a4_out[r], a_p1, (0, 0)), (send[r], f_p1, (0, 1))])

    @pl.when(info[s] > 3)
    def _():
        for r in ROLES:
            to, near, far = TOWARD[r], r, 1 - r
            i_h1, i_p0 = load(i3_out[r], 0, 0), load(i3_out[r], 0, 1)
            i_p1, i_p2 = load(i3p[r], 0, near), load(i3p[r], 0, far)
            w0 = [load(wb[r], 0, c, 1) for c in range(3)]
            w1 = [load(wp[r], 0, c, near) for c in range(3)]
            late(r, forward(i_p0, i_p1, i_h1, w0, to), forward(i_p1, i_p2, i_p0, w1, to))

    @pl.when(info[s] <= 3)
    def _():
        for r in ROLES:
            late(r, load(i3_out[r], 0, 1), load(i3p[r], 0, r))


def inner_3(info, s, *refs):
    w_in, wbz, wbc, s2z, s2c, a4z, a4c, a4_in, i3_in, i3z, i3c, i2_in, s1z, s1c, i1_in, i4_in, i4z, i4c = refs[:18]
    a3_in, a2_in, g_in, warped, a, f, x, sems = refs[18:]
    odd = info[4]

    def copies():
        def one(source, j):
            return pltpu.make_async_copy(source, warped.at[s, natural(odd, j)], sems.at[j])

        pairs = [(i4z.at[0, 0], 0), (i4z.at[0, 1], 1), (i4c.at[0, 1], 6), (i4c.at[0, 0], 7)]
        pairs += [(i4_in.at[0, j - 2], j) for j in range(2, 6)]
        return [one(source, j) for source, j in pairs]

    for copy in copies():
        copy.start()
    a[0], a[7] = s2z[0, 0], s2c[0, 0]
    a[1], a[6] = a4z[0, 0], a4c[0, 0]
    a[2:6] = a4_in[0]

    @pl.when(info[s] > 3)
    def _():
        x[0], x[7] = i3z[0, 1], i3c[0, 1]
        x[1:7] = i3_in[0]
        f[0] = wbz[0, 0, 1] * a[0]
        f[7] = wbc[0, 0, 1] * a[7]
        f[1:7] = w_in[0, 0] * a[1:7]

        def step(j, _):
            mid = load(a, j)
            wy, wx = (load(w_in, 0, c, j - 1) for c in (1, 2))
            adj = backward(mid, load(f, j + 1), load(f, j - 1), wy, wx)
            g = grads(mid, load(x, j), load(x, j + 1), load(x, j - 1))
            store_all([(a3_in, adj, (0, j - 1))] + [(g_in, g[c], (0, c, j - 1)) for c in range(3)])
            return 0

        unrolled(1, 7, step)

    @pl.when(info[s] <= 3)
    def _():
        a3_in[0] = a[1:7]
        g_in[...] = jnp.zeros(g_in.shape, f32)

    @pl.when(info[s] > 2)
    def _():
        gather_planes(x, (s1z, s1c), i2_in)
        f[1:7] = w_in[0, 0] * a3_in[0]

        def gradient(j, adj):
            g = grads(adj, load(x, j), load(x, j + 1), load(x, j - 1))
            return [(g_in, add(load(g_in, 0, c, j - 1), g[c]), (0, c, j - 1)) for c in range(3)]

        def end(i, _):
            j = 1 + 5 * i
            store_all(gradient(j, load(a3_in, 0, j - 1)))
            return 0

        unrolled(0, 2, end)

        def step(j, _):
            mid = load(a3_in, 0, j - 1)
            wy, wx = (load(w_in, 0, c, j - 1) for c in (1, 2))
            adj = backward(mid, load(f, j + 1), load(f, j - 1), wy, wx)
            store_all([(a2_in, adj, (0, j - 2))] + gradient(j, mid))
            return 0

        unrolled(2, 6, step)

    @pl.when(info[s] <= 2)
    def _():
        a2_in[0] = a3_in[0, 1:5]

    @pl.when(info[s] > 1)
    def _():
        def step(j, _):
            at = lambda i: load(i1_in, 0, i - 1)
            g = grads(load(a2_in, 0, j - 2), at(j), at(j + 1), at(j - 1))
            store_all([(g_in, add(load(g_in, 0, c, j - 1), g[c]), (0, c, j - 1)) for c in range(3)])
            return 0

        unrolled(2, 6, step)

    for copy in copies():
        copy.wait()


def outer_3(info, s, *refs):
    r2, wb, wp, s2, a3p, i3b, i3p, r1, s1, i1b, i1p = (refs[2 * i : 2 * i + 2] for i in range(11))
    a3, a2_out, send = (refs[22 + 2 * i : 24 + 2 * i] for i in range(3))

    def gz(r, adj, inner, outer):
        return (send[r], add(load(send[r], 0, 2), mul(adj, dz(inner, outer, TOWARD[r]))), (0, 2))


    @pl.when(info[s] > 3)
    def _():
        for r in ROLES:
            to = TOWARD[r]
            a_h1, a_p0 = load(r2[r], 0, 0), load(s2[r], 0, 0)
            f_h2, f_p1 = scale(load(r2[r], 0, 1), -1.0), load(s2[r], 0, 1)
            wh = [load(wb[r], 0, c, 0) for c in range(3)]
            w0 = [load(wb[r], 0, c, 1) for c in range(3)]
            store(a3[r], backward(a_h1, mul(w0[0], a_p0), f_h2, wh[1], wh[2], to), 0, 0)
            b_p0 = backward(a_p0, f_p1, mul(wh[0], a_h1), w0[1], w0[2], to)
            g = mul(a_p0, dz(load(i3p[r], 0, r), load(i3b[r], 0, 0), to))
            store_all([(a3[r], b_p0, (0, 1)), (send[r], g, (0, 2))])

    @pl.when(info[s] <= 3)
    def _():
        for r in ROLES:
            a3[r][0, 0] = r2[r][0, 0]
            a3[r][0, 1] = s2[r][0, 0]
            send[r][0, 2] = jnp.zeros(send[r].shape[2:], f32)

    def late(r, a2_p0, a2_p1):
        f_p1 = mul(load(wp[r], 0, 0, r), a2_p1)
        store_all([(a2_out[r], a2_p0, (0, 0)), (send[r], a2_p0, (0, 0))])
        store_all([(a2_out[r], a2_p1, (0, 1)), (send[r], f_p1, (0, 1))])

    @pl.when(info[s] > 2)
    def _():
        for r in ROLES:
            to, near, far = TOWARD[r], r, 1 - r
            a_h1, a_p0 = load(a3[r], 0, 0), load(a3[r], 0, 1)
            a_p1, a_p2 = load(a3p[r], 0, near), load(a3p[r], 0, far)
            wh0 = load(wb[r], 0, 0, 0)
            w0 = [load(wb[r], 0, c, 1) for c in range(3)]
            w1 = [load(wp[r], 0, c, near) for c in range(3)]
            f_p2 = mul(load(wp[r], 0, 0, far), a_p2)
            store_all([gz(r, a_p0, load(s1[r], 0, 1), load(r1[r], 0, 0))])
            late(
                r,
                backward(a_p0, mul(w1[0], a_p1), mul(wh0, a_h1), w0[1], w0[2], to),
                backward(a_p1, f_p2, mul(w0[0], a_p0), w1[1], w1[2], to),
            )

    @pl.when(info[s] <= 2)
    def _():
        for r in ROLES:
            late(r, load(a3[r], 0, 1), load(a3p[r], 0, r))

    @pl.when(info[s] > 1)
    def _():
        for r in ROLES:
            store_all([gz(r, load(a2_out[r], 0, 0), load(i1p[r], 0, r), load(i1b[r], 0, 0))])


def inner_4(info, s, *refs):
    w_in, wbz, wbc, a2_in, a2z, a2c, *rest, a1_in, total, g_full, gbz, gbc, a, f = refs
    gather_planes(a, (a2z, a2c), a2_in)

    @pl.when(s == 0)
    def _():
        total[...] = jnp.zeros(total.shape, f32)

    @pl.when(info[s] > 1)
    def _():
        f[0] = wbz[0, 0, 1] * a[0]
        f[7] = wbc[0, 0, 1] * a[7]
        f[1:7] = w_in[0, 0] * a[1:7]

        def step(j, _):
            mid = load(a, j)
            wy, wx = (load(w_in, 0, c, j - 1) for c in (1, 2))
            store(a1_in, backward(mid, load(f, j + 1), load(f, j - 1), wy, wx), 0, j - 1)
            return 0

        unrolled(1, 7, step)

    @pl.when(info[s] <= 1)
    def _():
        a1_in[0] = a[1:7]

    f[1:7] = w_in[0, 0] * a1_in[0]

    def last(j, _):
        mid = load(a1_in, 0, j - 1)
        wy, wx = (load(w_in, 0, c, j - 1) for c in (1, 2))
        adj = backward(mid, load(f, j + 1), load(f, j - 1), wy, wx)
        add_t(total, adj, j - 2)
        return 0

    unrolled(2, 6, last)
    r2, a3, s2, s3, i3b, i3p, r1, s1, i1b, i1p = (rest[2 * i : 2 * i + 2] for i in range(10))
    t, dt, g_in = rest[20:23]
    a2b, gb = (a2z, a2c), (gbz, gbc)

    def step(j, _):
        adj = load(a1_in, 0, j - 1)
        g = grads(adj, None, t_load(t, j + 1), t_load(t, j - 1), slopes=t_slopes(dt, j))
        store_all([(g_full, add(load(g_in, 0, c, j - 1), g[c]), (0, c, j - 1)) for c in range(3)])
        return 0

    unrolled(1, 7, step)
    for r in ROLES:
        to, near, far = TOWARD[r], r, 1 - r
        p1 = 0 if r == 0 else 5
        g = gb[r]

        def more(plane, parts, first=False):
            values = [(g, value if first else add(load(g, 0, c, plane), value), (0, c, plane)) for c, value in parts]
            store_all(values)

        def at_h1(adj, image):
            return [(1, mul(adj, dy(image))), (2, mul(adj, dx(image)))]

        def at_p0(adj, *images):
            return list(enumerate(grads(adj, *images, to)))[1:]

        @pl.when(info[s] > 3)
        def _():
            i_h1, i_p0 = load(i3b[r], 0, 0), load(i3b[r], 0, 1)
            more(0, at_h1(load(r2[r], 0, 0), i_h1), True)
            more(1, at_p0(load(s2[r], 0, 0), i_p0, load(i3p[r], 0, near), i_h1), True)

        @pl.when(info[s] <= 3)
        def _():
            g[...] = jnp.zeros(g.shape, f32)

        @pl.when(info[s] > 2)
        def _():
            i_h1, i_p0 = load(r1[r], 0, 0), load(s1[r], 0, 0)
            more(0, at_h1(load(a3[r], 0, 0), i_h1))
            more(1, at_p0(load(a3[r], 0, 1), i_p0, load(s1[r], 0, 1), i_h1))

        @pl.when(info[s] > 1)
        def _():
            i_h1, i_p0 = load(i1b[r], 0, 0), load(i1b[r], 0, 1)
            i_p1, i_p2 = load(i1p[r], 0, near), load(i1p[r], 0, far)
            more(1, at_p0(load(a2b[r], 0, 0), i_p0, i_p1, i_h1))
            g1 = grads(load(a2b[r], 0, 1), i_p1, i_p2, i_p0, to)
            store_all([(g_full, add(load(g_full, 0, c, p1), g1[c]), (0, c, p1)) for c in range(3)])

        g[0, 0, 1] = s3[r][0, 2]


def outer_4(info, s, *refs):
    r3, wb, wp, s3, a1p = (refs[2 * i : 2 * i + 2] for i in range(5))
    total_in, total_out, *outs = refs[10:14]
    total, a1s, sems = refs[14:]
    odd = info[4]

    def sent(r):
        return pltpu.make_async_copy(a1s.at[s, r], outs[r].at[s], sems.at[s, r])

    @pl.when(s == 0)
    def _():
        for j in range(2, 6):
            total[:, natural(odd, j)] = total_in[:, j - 2]
        for j in (0, 1, 6, 7):
            total[:, j] = jnp.zeros((8, 8, COLS), f32)

    for r in ROLES:
        to, near, far = TOWARD[r], r, 1 - r

        active = (info[s] > 1).astype(f32)
        a_h1, a_p0 = load(r3[r], 0, 0), load(s3[r], 0, 0)
        f_h2, f_p1 = scale(load(r3[r], 0, 1), -1.0), load(s3[r], 0, 1)
        wh = [load(wb[r], 0, c, 0) for c in range(3)]
        w0 = [load(wb[r], 0, c, 1) for c in range(3)]
        b_h1 = backward(a_h1, mul(w0[0], a_p0), f_h2, wh[1], wh[2], to, active)
        b_p0 = backward(a_p0, f_p1, mul(wh[0], a_h1), w0[1], w0[2], to, active)
        store_all([(a1s, b_h1, (s, r, 0)), (a1s, b_p0, (s, r, 1))])
        w1 = [load(wp[r], 0, c, near) for c in range(3)]
        b_p1, b_p2 = load(a1p[r], 0, near), load(a1p[r], 0, far)
        c_p0 = backward(b_p0, mul(w1[0], b_p1), mul(wh[0], b_h1), w0[1], w0[2], to)
        c_p1 = backward(b_p1, mul(load(wp[r], 0, 0, far), b_p2), mul(w0[0], b_p0), w1[1], w1[2], to)
        for k, value in enumerate((c_p0, c_p1)):
            add_t(total, value, natural(odd, k if r == 0 else 7 - k))
        sent(r).start()

    @pl.when(s == 3)
    def _():
        last = pltpu.make_async_copy(total, total_out, sems.at[4, 0])
        last.start()
        for at in range(4):
            for r in ROLES:
                pltpu.make_async_copy(a1s.at[at, r], outs[r].at[at], sems.at[at, r]).wait()
        last.wait()


def final(mid, inner, outer, turn):
    return smooth(mid, inner, outer, -half * centre * turn, -half * smoothing * turn)


def finish(info, s, *refs):
    r3, a1b, gb, i1b = (refs[2 * i : 2 * i + 2] for i in range(4))
    t, dt, g_full, mg, made, sems = refs[8:]
    odd = info[4]
    sign = (1 - 2 * odd).astype(f32)
    slot = lax.rem(s, 2)

    def copy_out(which, at):
        return pltpu.make_async_copy(made.at[which], mg.at[at], sems.at[which])

    @pl.when(s >= 2)
    def _():
        copy_out(slot, s - 2).wait()

    def step(j, _):
        for c in range(3):
            at = lambda i: load(g_full, 0, c, i - 1)
            store(made, final(at(j), at(j + 1), at(j - 1), sign if c == 0 else 1.0), slot, c, natural(odd, j))
        return 0

    unrolled(2, 6, step)
    for r in ROLES:
        to = TOWARD[r]
        p1, p2 = (0, 1) if r == 0 else (5, 4)
        n0, n1 = (natural(odd, k if r == 0 else 7 - k) for k in (0, 1))
        inside = info[5].astype(f32) if r == 0 else 1.0
        step_one = (info[s] > 1).astype(f32)
        th2, th1, tp0, tp1 = (t_load(t, k, r) for k in (-2, -1, 0, 1))
        slopes = t_slopes(dt, -1, r)
        a_one = scale(load(r3[r], 0, 0), step_one)
        i_h1 = load(i1b[r], 0, 0)
        b_h1, b_p0 = load(a1b[r], 0, 0), load(a1b[r], 0, 1)
        g_h1 = [
            add(scale(load(r3[r], 0, 2), -1.0), mul(b_h1, dz(tp0, th2, to))),
            add(load(gb[r], 0, 1, 0), mul(a_one, dy(i_h1)), mul(b_h1, slopes[0])),
            add(load(gb[r], 0, 2, 0), mul(a_one, dx(i_h1)), mul(b_h1, slopes[1])),
        ]
        g_p0 = grads(b_p0, tp0, tp1, th1, to, t_slopes(dt, 0, r))
        for c in range(3):
            turn = sign if c == 0 else 1.0
            g0 = add(load(gb[r], 0, c, 1), g_p0[c])
            g1, g2 = load(g_full, 0, c, p1), load(g_full, 0, c, p2)
            store(made, final(g0, g1, scale(g_h1[c], inside), turn), slot, c, n0)
            store(made, final(g1, g2, g0, turn), slot, c, n1)

    copy_out(slot, s).start()

    @pl.when(s == 3)
    def _():
        copy_out(1 - slot, s - 1).wait()
        copy_out(slot, s).wait()


ROWS, COLS = 64, 256
PLANE = (ROWS, COLS)


def one(ref, s):
    return ref.at[pl.ds(s, 1)]


def whole(ref, s):
    return ref


def stream(ref, s):
    return ref


def flows(view):
    return view is stream or getattr(view, "streamed", False)


def pair(at, streamed=False):
    def view(ref, s):
        subject = pl.ds(0 if streamed else s, 1)
        if len(ref.shape) == 5:
            return ref.at[subject, :, pl.ds(at, 2)]
        return ref.at[subject, pl.ds(at, 2)]

    view.streamed = streamed
    return view


def call(kernel, info, ins, outs, scratch=(), us=1.0, mib=5):
    arrays, places = [], []
    streams = any(flows(view) for _, view in list(ins) + list(outs))
    for array, _ in ins:
        known = [i for i, other in enumerate(arrays) if other is array]
        if not known:
            arrays.append(array)
        places.append(known[0] if known else len(arrays) - 1)
    subjects = 4

    def body(info_ref, *refs):
        given, made = refs[: len(arrays)], refs[len(arrays) : len(arrays) + len(outs)]

        def per(s, _):
            views = [view(given[at], s) for at, (_, view) in zip(places, ins)]
            views += [view(ref, s) if view else ref for ref, (_, view) in zip(made, outs)]
            kernel(info_ref, s, *views, *refs[len(arrays) + len(outs) :])
            return 0

        if streams:
            per(pl.program_id(0), 0)
        else:
            lax.fori_loop(0, subjects, per, 0)

    vmem = pl.BlockSpec(memory_space=pltpu.VMEM)

    def block(dims):
        return pl.BlockSpec((1,) + dims[1:], lambda s: (s,) + (0,) * (len(dims) - 1))

    def made_of(dims, view):
        if view is stream:
            return block(dims), pltpu.HBM(dims, f32)
        if view is None:
            return pl.BlockSpec(memory_space=pl.ANY), pltpu.HBM(dims, f32)
        return vmem, jax.ShapeDtypeStruct(dims, f32)

    streamed = [any(flows(view) for other, view in ins if other is array) for array in arrays]
    operands = [pltpu.with_memory_space_constraint(a, pltpu.HBM) if st else a for a, st in zip(arrays, streamed)]
    out_specs, out_shapes = zip(*(made_of(*o) for o in outs))

    return pl.pallas_call(
        body,
        grid=(subjects,) if streams else (),
        in_specs=[pl.BlockSpec(memory_space=pltpu.SMEM)] + [block(a.shape) if st else vmem for a, st in zip(arrays, streamed)],
        out_specs=list(out_specs),
        out_shape=list(out_shapes),
        scratch_shapes=list(scratch),
        compiler_params=pltpu.CompilerParams(vmem_limit_bytes=mib * 1024 * 1024),
        cost_estimate=pl.CostEstimate(flops=0, bytes_accessed=int(us * 3.3e6), transcendentals=0),
        name=kernel.__name__,
    )(info, *operands)


def shards(template, momentum, targets, step_count):
    count = lax.axis_size("space")
    groups = lax.axis_size("subj")
    place = lax.axis_index("space")
    odd = place % 2
    core_pairs = [(i, i ^ 1) for i in range(count)]
    chip_pairs = [(i, ((i + 1) ^ 1) - 1) for i in range(1, count - 1)]

    def swap(sides):
        return lax.ppermute(sides[0], "space", chip_pairs), lax.ppermute(sides[1], "space", core_pairs)

    group = lax.axis_index("subj")
    inside = jnp.logical_and(place > 0, place < count - 1)
    info = jnp.concatenate([step_count, jnp.stack([odd, inside, group]).astype(jnp.int32)])

    def ends(array, dim):
        return tuple(lax.dynamic_slice_in_dim(array, at, 2, dim) for at in (6 * odd, 6 - 6 * odd))

    def shape(*lead):
        return (step_count.shape[0],) + lead + PLANE

    def both(arrays, *views):
        return [(arrays[0], views[0]), (arrays[1], views[-1])]

    def near(array, streamed=False):
        return both((array, array), pair(0, streamed), pair(4, streamed))

    def out(*lead):
        return (shape(*lead), one)

    def out2(*lead):
        return [out(*lead)] * 2

    def planes(n):
        return pltpu.VMEM((n,) + PLANE, f32)

    def partner(array, by):
        return lax.ppermute(array, "subj", [(i, i ^ by) for i in range(groups)])

    across, ms = lax.optimization_barrier((partner(template, 1), ends(momentum, 2)))
    own = jnp.stack([template, across])
    t_halo, ms = lax.optimization_barrier((swap(ends(own, 1)), ms))
    mr = swap(ms)
    wide = jnp.concatenate([t_halo[0], own, t_halo[1]], axis=1)
    wide, late_info = lax.optimization_barrier((wide, info))
    rows = [wide] + [partner(wide, by) for by in (2, 4, 6)]
    w_in, w_edge, m_edge = call(
        velocity_inner, late_info, [(momentum, stream)], [out(3, 6), out(3, 2), out(3, 2)], us=5
    )
    t, dt = call(
        template_planes, info, [(x, whole) for x in rows], [((12,) + PLANE, whole), ((2, 10) + PLANE, whole)], us=1
    )
    tdt = [(t, whole), (dt, whole)]
    i1_in, i2_in = call(inner_1, info, [(w_in, one)] + tdt, [out(6), out(4)], us=3)
    *made, s1z, s1c = call(
        outer_1,
        info,
        both(mr, stream) + [(m_edge, one), (w_edge, one)] + tdt + near(w_in) + near(i1_in),
        out2(3, 2) + out2(2) + out2(2),
        us=5,
    )
    wb, i1b = made[:2], made[2:]
    s1 = (s1z, s1c)
    r1 = swap(s1)
    i3_in, i4_in, a4_in = call(
        inner_2,
        info,
        [(w_in, one), (i2_in, one)] + both(s1, one) + [(targets, one)],
        [out(6), out(4), out(4)],
        [planes(8)],
        us=4,
    )
    made = call(
        outer_2,
        info,
        both(r1, one) + both(wb, one) + near(w_in) + both(s1, one) + near(i3_in) + [(targets, one)],
        out2(2) + out2(2) + out2(1) + out2(2),
        us=3,
    )
    i3b, i4b, a4b, s2 = (made[2 * i : 2 * i + 2] for i in range(4))
    r2 = swap(s2)
    a3_in, a2_in, g_in, warped = call(
        inner_3,
        info,
        [(w_in, one)]
        + both(wb, one)
        + both(s2, one)
        + both(a4b, one)
        + [(a4_in, one), (i3_in, one)]
        + both(i3b, one)
        + [(i2_in, one)]
        + both(s1, one)
        + [(i1_in, one), (i4_in, one)]
        + both(i4b, one),
        [out(6), out(4), out(3, 6), (shape(8), None)],
        [planes(8)] * 3 + [pltpu.SemaphoreType.DMA((8,))],
        us=7,
    )
    images = both(i3b, one) + near(i3_in) + both(r1, one) + both(s1, one) + both(i1b, one) + near(i1_in)
    made = call(
        outer_3,
        info,
        both(r2, one) + both(wb, one) + near(w_in) + both(s2, one) + near(a3_in) + images,
        out2(2) + out2(2) + out2(3),
        us=2,
    )
    a3b, a2b, s3 = (made[2 * i : 2 * i + 2] for i in range(3))
    r3 = swap(s3)
    small, tile = (groups, 4, 8, COLS), (groups, 8, 8, COLS)
    a1_in, total, g_full, *gb = call(
        inner_4,
        info,
        [(w_in, one)]
        + both(wb, one)
        + [(a2_in, one)]
        + both(a2b, one)
        + both(r2, one)
        + both(a3b, one)
        + both(s2, one)
        + both(s3, one)
        + images
        + tdt
        + [(g_in, one)],
        [out(6), (small, whole), out(3, 6)] + out2(3, 2),
        [planes(8)] * 2,
        us=5,
    )
    total, *a1b = call(
        outer_4,
        info,
        both(r3, one) + both(wb, one) + near(w_in) + both(s3, one) + near(a1_in) + [(total, whole)],
        [(tile, None)] + [(shape(2), None)] * 2,
        [pltpu.VMEM(tile, f32), pltpu.VMEM((4, 2, 2) + PLANE, f32), pltpu.SemaphoreType.DMA((5, 2))],
        us=3,
    )
    parts = lax.all_to_all(total, "subj", 0, 0)
    (momentum_gradient,) = call(
        finish,
        info,
        both(r3, stream) + both(a1b, stream) + both(gb, stream) + both(i1b, stream) + tdt + [(g_full, stream)],
        [(shape(3, 8), None)],
        [pltpu.VMEM((2, 3, 8) + PLANE, f32), pltpu.SemaphoreType.DMA((2,))],
        us=6,
        mib=14,
    )
    template_gradient = jnp.sum(parts, axis=0)
    return (warped, template_gradient, momentum_gradient)


def solution(mesh):
    in_specs = (
        P("space", "subj", None),
        P("subj", None, "space", None, None),
        P("subj", "space", None, None),
        P("subj"),
    )
    out_specs = (
        P("subj", "space", None, None),
        P("space", "subj", None),
        P("subj", None, "space", None, None),
    )
    return jax.shard_map(shards, mesh=mesh, in_specs=in_specs, out_specs=out_specs, check_vma=False)
```

```python
import jax
import jax.numpy as jnp
from jax import lax
from jax.experimental import pallas as pl
from jax.experimental.pallas import tpu as pltpu
from jax.sharding import PartitionSpec as P

time_step = 0.15
smoothing = 0.1
half = 0.5 * time_step
centre = 1.0 - 6.0 * smoothing
f32 = jnp.float32


class Plane:
    def __init__(self, rows):
        self.rows, self.known, self.rolled = rows, {}, {}

    def at(self, b):
        if b not in self.known:
            self.known[b] = tuple(self.rows(b))
        return self.known[b]

    def turned(self, b, by):
        if (b, by) not in self.rolled:
            self.rolled[b, by] = tuple(pltpu.roll(x, by, axis=0) for x in self.at(b))
        return self.rolled[b, by]


BLOCKS = 8


def halves(h):
    return pl.ds(128 * h, 128)


def load(ref, *at):
    return Plane(lambda b: [ref[at + (pl.ds(8 * b, 8), halves(h))] for h in (0, 1)])


def store(ref, plane, *at):
    store_all([(ref, plane, at)])


def store_all(targets):
    for b in range(BLOCKS):
        for ref, plane, at in targets:
            for h, value in enumerate(plane.at(b)):
                ref[at + (pl.ds(8 * b, 8), halves(h))] = value


def add_t(ref, plane, p):
    for b in range(BLOCKS):
        for h, value in enumerate(plane.at(b)):
            ref[b, p, :, halves(h)] += value


def each(fn, *planes):
    return Plane(lambda b: [fn(*x) for x in zip(*(plane.at(b) for plane in planes))])


def add(*planes):
    total = planes[0]
    for plane in planes[1:]:
        total = each(lambda a, b: a + b, total, plane)
    return total


def sub(a, b):
    return each(lambda x, y: x - y, a, b)


def mul(a, b):
    return each(lambda x, y: x * y, a, b)


def scale(a, factor):
    return each(lambda x: x * factor, a)


def y_sides(plane):
    def rows(b, by, edge, step):
        row = lax.broadcasted_iota(jnp.int32, (8, 128), 0)
        here, there = plane.turned(b, by), b + step
        over = plane.turned(there, by) if 0 <= there < BLOCKS else (0.0, 0.0)
        return [jnp.where(row == edge, o, x) for o, x in zip(over, here)]

    return Plane(lambda b: rows(b, 1, 0, -1)), Plane(lambda b: rows(b, 7, 7, 1))


def x_sides(plane):
    def before(b):
        lane = lax.broadcasted_iota(jnp.int32, (8, 128), 1)
        left, right = (pltpu.roll(x, 1, axis=1) for x in plane.at(b))
        return jnp.where(lane == 0, 0.0, left), jnp.where(lane == 0, left, right)

    def after(b):
        lane = lax.broadcasted_iota(jnp.int32, (8, 128), 1)
        left, right = (pltpu.roll(x, 127, axis=1) for x in plane.at(b))
        return jnp.where(lane == 127, right, left), jnp.where(lane == 127, 0.0, right)

    return Plane(before), Plane(after)


def dy(plane):
    before, after = y_sides(plane)
    return sub(after, before)


def dx(plane):
    before, after = x_sides(plane)
    return sub(after, before)


def smooth(mid, inner, outer, a, b):
    total = add(*(plane for plane in (inner, outer) if plane is not None), *y_sides(mid), *x_sides(mid))
    return each(lambda m, t: a * m + b * t, mid, total)


def dz(inner, outer, toward):
    return sub(inner, outer) if toward > 0 else sub(outer, inner)


def forward(mid, inner, outer, w, toward=1):
    change = add(mul(w[0], dz(inner, outer, toward)), mul(w[1], dy(mid)), mul(w[2], dx(mid)))
    return sub(mid, change)


def forward_by(mid, inner, outer, slopes, w, toward=1):
    change = add(mul(w[0], dz(inner, outer, toward)), mul(w[1], slopes[0]), mul(w[2], slopes[1]))
    return sub(mid, change)


def backward(mid, flux_inner, flux_outer, wy, wx, toward=1, active=None):
    change = add(dz(flux_inner, flux_outer, toward), dy(mul(wy, mid)), dx(mul(wx, mid)))
    return add(mid, change if active is None else scale(change, active))


def grads(adj, mid, inner, outer, toward=1, slopes=None):
    sy, sx = slopes or (dy(mid), dx(mid))
    return [mul(adj, dz(inner, outer, toward)), mul(adj, sy), mul(adj, sx)]


def natural(odd, j):
    return j + odd * (7 - 2 * j)


def unrolled(low, high, step):
    for j in range(low, high):
        step(j, 0)


ROLES = (0, 1)
TOWARD = (1, -1)


def t_load(t, k, role=0):
    return load(t, k if role == 0 else 7 - k)


def t_slopes(dt, k, role=0):
    return [load(dt, c, k if role == 0 else 7 - k) for c in (0, 1)]


def named(kernel, name, role):
    kernel.__name__ = name + ("_chip", "_core")[role]
    return kernel


def halo_slopes(s, th, slopes, roles=ROLES):
    @pl.when(s == 0)
    def _():
        for r in roles:
            mid = load(th[r], 0)
            store_all([(slopes, dy(mid), (r, 0)), (slopes, dx(mid), (r, 1))])

    return {r: [load(slopes, r, c) for c in (0, 1)] for r in roles}


def template_planes(info, s, *refs):
    *sources, t, dt, send_z, send_c = refs
    odd, me = info[4], info[6]

    @pl.when(s == 0)
    def _():
        for j in range(8):
            for i, source in enumerate(sources):
                for x in (0, 1):
                    row = pl.multiple_of(8 * jnp.bitwise_xor(me, 2 * i + x), 8)
                    t[j, pl.ds(row, 8)] = source[x, natural(odd, j)]
        for i in (0, 1):
            send_z[i] = t[i]
            send_c[i] = t[7 - i]
        for j in range(8):
            mid = load(t, j)
            store_all([(dt, dy(mid), (0, j)), (dt, dx(mid), (1, j))])


def velocity_inner(info, s, m, w_in, w_edge, m_edge):
    odd = info[4]
    sign = (1 - 2 * odd).astype(f32)
    for j in range(8):
        for c in range(3):
            turn = sign if c == 0 else 1.0
            v = smooth(
                load(m, 0, c, natural(odd, j)),
                load(m, 0, c, natural(odd, j + 1)) if j < 7 else None,
                load(m, 0, c, natural(odd, j - 1)) if j > 0 else None,
                half * centre * turn,
                half * smoothing * turn,
            )
            if 0 < j < 7:
                store(w_in, v, 0, c, j - 1)
            else:
                store(w_edge, v, 0, c, j // 7)
                m_edge[0, c, j // 7] = m[0, c, natural(odd, j)]


def inner_1(info, s, w_in, t, dt, i1_in, i2_in):
    def first(j, _):
        w = [load(w_in, 0, c, j - 1) for c in range(3)]
        image = forward_by(t_load(t, j), t_load(t, j + 1), t_load(t, j - 1), t_slopes(dt, j), w)
        store(i1_in, image, 0, j - 1)
        return 0

    unrolled(1, 7, first)

    @pl.when(info[s] > 1)
    def _():
        def second(j, _):
            at = lambda i: load(i1_in, 0, i - 1)
            w = [load(w_in, 0, c, j - 1) for c in range(3)]
            store(i2_in, forward(at(j), at(j + 1), at(j - 1), w), 0, j - 2)
            return 0

        unrolled(2, 6, second)

    @pl.when(info[s] <= 1)
    def _():
        i2_in[0] = i1_in[0, 1:5]


def outer_1(role):
    roles = (role,)

    def kernel(info, s, *refs):
        m_edge, w_edge, t, dt = refs[:4]
        mr, th, wp, i1p, w_out, i1_out, send = ({role: ref} for ref in refs[4:11])
        slopes = halo_slopes(s, th, refs[11], roles)
        odd = info[4]
        sign = (1 - 2 * odd).astype(f32)
        for r in roles:
            to = TOWARD[r]
            h1 = 1 - odd if r == 0 else odd
            inside = info[5].astype(f32) if r == 0 else 1.0
            wh, w0 = [], []
            for c in range(3):
                turn = sign if c == 0 else 1.0
                m_h1, m_p0 = load(mr[r], 0, c, h1), load(m_edge, 0, c, r)
                a, b = half * centre * turn, half * smoothing * turn
                wh.append(smooth(m_h1, m_p0, load(mr[r], 0, c, 1 - h1), a * inside, b * inside))
                w0.append(add(load(w_edge, 0, c, r), scale(m_h1, b)))
            th1, th2, tp0, tp1 = load(th[r], 0), load(th[r], 1), t_load(t, 0, r), t_load(t, 1, r)
            i_h1 = forward_by(th1, tp0, th2, slopes[r], wh, to)
            i_p0 = forward_by(tp0, tp1, th1, t_slopes(dt, 0, r), w0, to)
            targets = [(i1_out[r], i_h1, (0, 0)), (i1_out[r], i_p0, (0, 1))]
            targets += [(w_out[r], w[c], (0, c, i)) for i, w in enumerate((wh, w0)) for c in range(3)]
            store_all(targets)

        @pl.when(info[s] > 1)
        def _():
            for r in roles:
                to, near, far = TOWARD[r], r, 1 - r
                i_h1, i_p0 = load(i1_out[r], 0, 0), load(i1_out[r], 0, 1)
                i_p1, i_p2 = load(i1p[r], 0, near), load(i1p[r], 0, far)
                w0 = [load(w_out[r], 0, c, 1) for c in range(3)]
                w1 = [load(wp[r], 0, c, near) for c in range(3)]
                store(send[r], forward(i_p0, i_p1, i_h1, w0, to), 0, 0)
                store(send[r], forward(i_p1, i_p2, i_p0, w1, to), 0, 1)

        @pl.when(info[s] <= 1)
        def _():
            for r in roles:
                send[r][0, 0] = i1_out[r][0, 1]
                send[r][0, 1] = i1p[r][0, r]

    return named(kernel, "outer_1", role)


def gather_planes(x, sides, inner):
    x[0] = sides[0][0, 0]
    x[1] = sides[0][0, 1]
    x[7] = sides[1][0, 0]
    x[6] = sides[1][0, 1]
    x[2:6] = inner[0]


def inner_2(info, s, w_in, i2_in, s1z, s1c, targets, i3_in, i4_in, a4_in, x):
    odd = info[4]
    gather_planes(x, (s1z, s1c), i2_in)

    @pl.when(info[s] > 2)
    def _():
        def step(j, _):
            w = [load(w_in, 0, c, j - 1) for c in range(3)]
            store(i3_in, forward(load(x, j), load(x, j + 1), load(x, j - 1), w), 0, j - 1)
            return 0

        unrolled(1, 7, step)

    @pl.when(info[s] <= 2)
    def _():
        i3_in[0] = x[1:7]

    @pl.when(info[s] > 3)
    def _():
        def step(j, _):
            at = lambda i: load(i3_in, 0, i - 1)
            w = [load(w_in, 0, c, j - 1) for c in range(3)]
            image = forward(at(j), at(j + 1), at(j - 1), w)
            late = sub(image, load(targets, 0, natural(odd, j)))
            store_all([(i4_in, image, (0, j - 2)), (a4_in, late, (0, j - 2))])
            return 0

        unrolled(2, 6, step)

    @pl.when(info[s] <= 3)
    def _():
        def step(j, _):
            image = load(i3_in, 0, j - 1)
            late = sub(image, load(targets, 0, natural(odd, j)))
            store_all([(i4_in, image, (0, j - 2)), (a4_in, late, (0, j - 2))])
            return 0

        unrolled(2, 6, step)


def outer_2(role):
    roles = (role,)

    def kernel(info, s, *refs):
        targets = refs[0]
        r1, wb, wp, s1, i3p, i3_out, i4_out, a4_out, send = ({role: ref} for ref in refs[1:])
        odd = info[4]

        @pl.when(info[s] > 2)
        def _():
            for r in roles:
                i_h1, i_h2 = load(r1[r], 0, 0), load(r1[r], 0, 1)
                i_p0, i_p1 = load(s1[r], 0, 0), load(s1[r], 0, 1)
                wh = [load(wb[r], 0, c, 0) for c in range(3)]
                w0 = [load(wb[r], 0, c, 1) for c in range(3)]
                store(i3_out[r], forward(i_h1, i_p0, i_h2, wh, TOWARD[r]), 0, 0)
                store(i3_out[r], forward(i_p0, i_p1, i_h1, w0, TOWARD[r]), 0, 1)

        @pl.when(info[s] <= 2)
        def _():
            for r in roles:
                i3_out[r][0, 0] = r1[r][0, 0]
                i3_out[r][0, 1] = s1[r][0, 0]

        def late(r, i4_p0, i4_p1):
            n = [natural(odd, k if r == 0 else 7 - k) for k in (0, 1)]
            a_p0, a_p1 = sub(i4_p0, load(targets, 0, n[0])), sub(i4_p1, load(targets, 0, n[1]))
            store_all([(i4_out[r], i4_p0, (0, 0)), (send[r], a_p0, (0, 0))])
            f_p1 = mul(load(wp[r], 0, 0, r), a_p1)
            store_all([(i4_out[r], i4_p1, (0, 1)), (a4_out[r], a_p1, (0, 0)), (send[r], f_p1, (0, 1))])

        @pl.when(info[s] > 3)
        def _():
            for r in roles:
                to, near, far = TOWARD[r], r, 1 - r
                i_h1, i_p0 = load(i3_out[r], 0, 0), load(i3_out[r], 0, 1)
                i_p1, i_p2 = load(i3p[r], 0, near), load(i3p[r], 0, far)
                w0 = [load(wb[r], 0, c, 1) for c in range(3)]
                w1 = [load(wp[r], 0, c, near) for c in range(3)]
                late(r, forward(i_p0, i_p1, i_h1, w0, to), forward(i_p1, i_p2, i_p0, w1, to))

        @pl.when(info[s] <= 3)
        def _():
            for r in roles:
                late(r, load(i3_out[r], 0, 1), load(i3p[r], 0, r))

    return named(kernel, "outer_2", role)


def inner_3(info, s, *refs):
    w_in, wbz, wbc, s2z, s2c, a4z, a4c, a4_in, i3_in, i3z, i3c, i2_in, s1z, s1c, i1_in, i4_in, i4z, i4c = refs[:18]
    a3_in, a2_in, g_in, warped, a, f, x, sems = refs[18:]
    odd = info[4]

    def copies():
        def one(source, j):
            return pltpu.make_async_copy(source, warped.at[s, natural(odd, j)], sems.at[j])

        pairs = [(i4z.at[0, 0], 0), (i4z.at[0, 1], 1), (i4c.at[0, 1], 6), (i4c.at[0, 0], 7)]
        pairs += [(i4_in.at[0, j - 2], j) for j in range(2, 6)]
        return [one(source, j) for source, j in pairs]

    for copy in copies():
        copy.start()
    a[0], a[7] = s2z[0, 0], s2c[0, 0]
    a[1], a[6] = a4z[0, 0], a4c[0, 0]
    a[2:6] = a4_in[0]

    @pl.when(info[s] > 3)
    def _():
        x[0], x[7] = i3z[0, 1], i3c[0, 1]
        x[1:7] = i3_in[0]
        f[0] = wbz[0, 0, 1] * a[0]
        f[7] = wbc[0, 0, 1] * a[7]
        f[1:7] = w_in[0, 0] * a[1:7]

        def step(j, _):
            mid = load(a, j)
            wy, wx = (load(w_in, 0, c, j - 1) for c in (1, 2))
            adj = backward(mid, load(f, j + 1), load(f, j - 1), wy, wx)
            g = grads(mid, load(x, j), load(x, j + 1), load(x, j - 1))
            store_all([(a3_in, adj, (0, j - 1))] + [(g_in, g[c], (0, c, j - 1)) for c in range(3)])
            return 0

        unrolled(1, 7, step)

    @pl.when(info[s] <= 3)
    def _():
        a3_in[0] = a[1:7]
        g_in[...] = jnp.zeros(g_in.shape, f32)

    @pl.when(info[s] > 2)
    def _():
        gather_planes(x, (s1z, s1c), i2_in)
        f[1:7] = w_in[0, 0] * a3_in[0]

        def gradient(j, adj):
            g = grads(adj, load(x, j), load(x, j + 1), load(x, j - 1))
            return [(g_in, add(load(g_in, 0, c, j - 1), g[c]), (0, c, j - 1)) for c in range(3)]

        def end(i, _):
            j = 1 + 5 * i
            store_all(gradient(j, load(a3_in, 0, j - 1)))
            return 0

        unrolled(0, 2, end)

        def step(j, _):
            mid = load(a3_in, 0, j - 1)
            wy, wx = (load(w_in, 0, c, j - 1) for c in (1, 2))
            adj = backward(mid, load(f, j + 1), load(f, j - 1), wy, wx)
            store_all([(a2_in, adj, (0, j - 2))] + gradient(j, mid))
            return 0

        unrolled(2, 6, step)

    @pl.when(info[s] <= 2)
    def _():
        a2_in[0] = a3_in[0, 1:5]

    @pl.when(info[s] > 1)
    def _():
        def step(j, _):
            at = lambda i: load(i1_in, 0, i - 1)
            g = grads(load(a2_in, 0, j - 2), at(j), at(j + 1), at(j - 1))
            store_all([(g_in, add(load(g_in, 0, c, j - 1), g[c]), (0, c, j - 1)) for c in range(3)])
            return 0

        unrolled(2, 6, step)

    for copy in copies():
        copy.wait()


def outer_3(role):
    roles = (role,)

    def kernel(info, s, *refs):
        r2, wb, wp, s2, a3p, i3b, i3p, r1, s1, i1b, i1p, a3, a2_out, send = ({role: ref} for ref in refs)

        def gz(r, adj, inner, outer):
            return (send[r], add(load(send[r], 0, 2), mul(adj, dz(inner, outer, TOWARD[r]))), (0, 2))


        @pl.when(info[s] > 3)
        def _():
            for r in roles:
                to = TOWARD[r]
                a_h1, a_p0 = load(r2[r], 0, 0), load(s2[r], 0, 0)
                f_h2, f_p1 = scale(load(r2[r], 0, 1), -1.0), load(s2[r], 0, 1)
                wh = [load(wb[r], 0, c, 0) for c in range(3)]
                w0 = [load(wb[r], 0, c, 1) for c in range(3)]
                store(a3[r], backward(a_h1, mul(w0[0], a_p0), f_h2, wh[1], wh[2], to), 0, 0)
                b_p0 = backward(a_p0, f_p1, mul(wh[0], a_h1), w0[1], w0[2], to)
                g = mul(a_p0, dz(load(i3p[r], 0, r), load(i3b[r], 0, 0), to))
                store_all([(a3[r], b_p0, (0, 1)), (send[r], g, (0, 2))])

        @pl.when(info[s] <= 3)
        def _():
            for r in roles:
                a3[r][0, 0] = r2[r][0, 0]
                a3[r][0, 1] = s2[r][0, 0]
                send[r][0, 2] = jnp.zeros(send[r].shape[2:], f32)

        def late(r, a2_p0, a2_p1):
            f_p1 = mul(load(wp[r], 0, 0, r), a2_p1)
            store_all([(a2_out[r], a2_p0, (0, 0)), (send[r], a2_p0, (0, 0))])
            store_all([(a2_out[r], a2_p1, (0, 1)), (send[r], f_p1, (0, 1))])

        @pl.when(info[s] > 2)
        def _():
            for r in roles:
                to, near, far = TOWARD[r], r, 1 - r
                a_h1, a_p0 = load(a3[r], 0, 0), load(a3[r], 0, 1)
                a_p1, a_p2 = load(a3p[r], 0, near), load(a3p[r], 0, far)
                wh0 = load(wb[r], 0, 0, 0)
                w0 = [load(wb[r], 0, c, 1) for c in range(3)]
                w1 = [load(wp[r], 0, c, near) for c in range(3)]
                f_p2 = mul(load(wp[r], 0, 0, far), a_p2)
                store_all([gz(r, a_p0, load(s1[r], 0, 1), load(r1[r], 0, 0))])
                late(
                    r,
                    backward(a_p0, mul(w1[0], a_p1), mul(wh0, a_h1), w0[1], w0[2], to),
                    backward(a_p1, f_p2, mul(w0[0], a_p0), w1[1], w1[2], to),
                )

        @pl.when(info[s] <= 2)
        def _():
            for r in roles:
                late(r, load(a3[r], 0, 1), load(a3p[r], 0, r))

        @pl.when(info[s] > 1)
        def _():
            for r in roles:
                store_all([gz(r, load(a2_out[r], 0, 0), load(i1p[r], 0, r), load(i1b[r], 0, 0))])

    return named(kernel, "outer_3", role)


def inner_4(info, s, *refs):
    w_in, wbz, wbc, a2_in, a2z, a2c, *rest, a1_in, total, g_full, gbz, gbc, a, f = refs
    gather_planes(a, (a2z, a2c), a2_in)

    @pl.when(s == 0)
    def _():
        total[...] = jnp.zeros(total.shape, f32)

    @pl.when(info[s] > 1)
    def _():
        f[0] = wbz[0, 0, 1] * a[0]
        f[7] = wbc[0, 0, 1] * a[7]
        f[1:7] = w_in[0, 0] * a[1:7]

        def step(j, _):
            mid = load(a, j)
            wy, wx = (load(w_in, 0, c, j - 1) for c in (1, 2))
            store(a1_in, backward(mid, load(f, j + 1), load(f, j - 1), wy, wx), 0, j - 1)
            return 0

        unrolled(1, 7, step)

    @pl.when(info[s] <= 1)
    def _():
        a1_in[0] = a[1:7]

    f[1:7] = w_in[0, 0] * a1_in[0]

    def last(j, _):
        mid = load(a1_in, 0, j - 1)
        wy, wx = (load(w_in, 0, c, j - 1) for c in (1, 2))
        adj = backward(mid, load(f, j + 1), load(f, j - 1), wy, wx)
        add_t(total, adj, j - 2)
        return 0

    unrolled(2, 6, last)
    r2, a3, s2, s3, i3b, i3p, r1, s1, i1b, i1p = (rest[2 * i : 2 * i + 2] for i in range(10))
    t, dt, g_in = rest[20:23]
    a2b, gb = (a2z, a2c), (gbz, gbc)

    def step(j, _):
        adj = load(a1_in, 0, j - 1)
        g = grads(adj, None, t_load(t, j + 1), t_load(t, j - 1), slopes=t_slopes(dt, j))
        store_all([(g_full, add(load(g_in, 0, c, j - 1), g[c]), (0, c, j - 1)) for c in range(3)])
        return 0

    unrolled(1, 7, step)
    for r in ROLES:
        to, near, far = TOWARD[r], r, 1 - r
        p1 = 0 if r == 0 else 5
        g = gb[r]

        def more(plane, parts, first=False):
            values = [(g, value if first else add(load(g, 0, c, plane), value), (0, c, plane)) for c, value in parts]
            store_all(values)

        def at_h1(adj, image):
            return [(1, mul(adj, dy(image))), (2, mul(adj, dx(image)))]

        def at_p0(adj, *images):
            return list(enumerate(grads(adj, *images, to)))[1:]

        @pl.when(info[s] > 3)
        def _():
            i_h1, i_p0 = load(i3b[r], 0, 0), load(i3b[r], 0, 1)
            more(0, at_h1(load(r2[r], 0, 0), i_h1), True)
            more(1, at_p0(load(s2[r], 0, 0), i_p0, load(i3p[r], 0, near), i_h1), True)

        @pl.when(info[s] <= 3)
        def _():
            g[...] = jnp.zeros(g.shape, f32)

        @pl.when(info[s] > 2)
        def _():
            i_h1, i_p0 = load(r1[r], 0, 0), load(s1[r], 0, 0)
            more(0, at_h1(load(a3[r], 0, 0), i_h1))
            more(1, at_p0(load(a3[r], 0, 1), i_p0, load(s1[r], 0, 1), i_h1))

        @pl.when(info[s] > 1)
        def _():
            i_h1, i_p0 = load(i1b[r], 0, 0), load(i1b[r], 0, 1)
            i_p1, i_p2 = load(i1p[r], 0, near), load(i1p[r], 0, far)
            more(1, at_p0(load(a2b[r], 0, 0), i_p0, i_p1, i_h1))
            g1 = grads(load(a2b[r], 0, 1), i_p1, i_p2, i_p0, to)
            store_all([(g_full, add(load(g_full, 0, c, p1), g1[c]), (0, c, p1)) for c in range(3)])

        g[0, 0, 1] = s3[r][0, 2]


def outer_4(role):
    to, near, far = TOWARD[role], role, 1 - role

    def kernel(info, s, *refs):
        r3, wb, wp, s3, a1p, total_in, total_out, a1_out = refs[:8]
        total, a1s, sems = refs[8:]
        odd = info[4]
        first = 2 - 2 * odd

        def sent(at):
            return pltpu.make_async_copy(a1s.at[at], a1_out.at[at], sems.at[at])

        def six():
            return pltpu.make_async_copy(total_in, total_out.at[:, pl.ds(first, 6)], sems.at[4])

        @pl.when(s == 0)
        def _():
            if role == 0:
                six().start()
                total[...] = jnp.zeros(total.shape, f32)
            else:
                for j in range(2, 6):
                    total_out[:, natural(odd, j) - first] = total_in[:, j - 2]
                for j in (6, 7):
                    total_out[:, natural(odd, j) - first] = jnp.zeros((8, 8, COLS), f32)

        active = (info[s] > 1).astype(f32)
        a_h1, a_p0 = load(r3, 0, 0), load(s3, 0, 0)
        f_h2, f_p1 = scale(load(r3, 0, 1), -1.0), load(s3, 0, 1)
        wh = [load(wb, 0, c, 0) for c in range(3)]
        w0 = [load(wb, 0, c, 1) for c in range(3)]
        b_h1 = backward(a_h1, mul(w0[0], a_p0), f_h2, wh[1], wh[2], to, active)
        b_p0 = backward(a_p0, f_p1, mul(wh[0], a_h1), w0[1], w0[2], to, active)
        store_all([(a1s, b_h1, (s, 0)), (a1s, b_p0, (s, 1))])
        sent(s).start()
        w1 = [load(wp, 0, c, near) for c in range(3)]
        b_p1, b_p2 = load(a1p, 0, near), load(a1p, 0, far)
        c_p0 = backward(b_p0, mul(w1[0], b_p1), mul(wh[0], b_h1), w0[1], w0[2], to)
        c_p1 = backward(b_p1, mul(load(wp, 0, 0, far), b_p2), mul(w0[0], b_p0), w1[1], w1[2], to)
        for k, value in enumerate((c_p0, c_p1)):
            if role == 0:
                add_t(total, value, natural(odd, k) - 6 * odd)
            else:
                add_t(total_out, value, natural(odd, 7 - k) - first)

        @pl.when(s == 3)
        def _():
            if role == 0:
                last = pltpu.make_async_copy(total, total_out.at[:, pl.ds(6 * odd, 2)], sems.at[5])
                last.start()
                last.wait()
                six().wait()
            for at in range(4):
                sent(at).wait()

    return named(kernel, "outer_4", role)


def final(mid, inner, outer, turn):
    return smooth(mid, inner, outer, -half * centre * turn, -half * smoothing * turn)


def finish(info, s, *refs):
    r3, a1b, gb, i1b = (refs[2 * i : 2 * i + 2] for i in range(4))
    th, (t, dt, g_full, mg, made, sems, halo) = refs[8:10], refs[10:]
    slopes_h1 = halo_slopes(s, th, halo)
    odd = info[4]
    sign = (1 - 2 * odd).astype(f32)
    slot = lax.rem(s, 2)

    def copy_out(which, at):
        return pltpu.make_async_copy(made.at[which], mg.at[at], sems.at[which])

    @pl.when(s >= 2)
    def _():
        copy_out(slot, s - 2).wait()

    def step(j, _):
        for c in range(3):
            at = lambda i: load(g_full, 0, c, i - 1)
            store(made, final(at(j), at(j + 1), at(j - 1), sign if c == 0 else 1.0), slot, c, natural(odd, j))
        return 0

    unrolled(2, 6, step)
    for r in ROLES:
        to = TOWARD[r]
        p1, p2 = (0, 1) if r == 0 else (5, 4)
        n0, n1 = (natural(odd, k if r == 0 else 7 - k) for k in (0, 1))
        inside = info[5].astype(f32) if r == 0 else 1.0
        step_one = (info[s] > 1).astype(f32)
        th1, th2, tp0, tp1 = load(th[r], 0), load(th[r], 1), t_load(t, 0, r), t_load(t, 1, r)
        slopes = slopes_h1[r]
        a_one = scale(load(r3[r], 0, 0), step_one)
        i_h1 = load(i1b[r], 0, 0)
        b_h1, b_p0 = load(a1b[r], 0, 0), load(a1b[r], 0, 1)
        g_h1 = [
            add(scale(load(r3[r], 0, 2), -1.0), mul(b_h1, dz(tp0, th2, to))),
            add(load(gb[r], 0, 1, 0), mul(a_one, dy(i_h1)), mul(b_h1, slopes[0])),
            add(load(gb[r], 0, 2, 0), mul(a_one, dx(i_h1)), mul(b_h1, slopes[1])),
        ]
        g_p0 = grads(b_p0, tp0, tp1, th1, to, t_slopes(dt, 0, r))
        for c in range(3):
            turn = sign if c == 0 else 1.0
            g0 = add(load(gb[r], 0, c, 1), g_p0[c])
            g1, g2 = load(g_full, 0, c, p1), load(g_full, 0, c, p2)
            store(made, final(g0, g1, scale(g_h1[c], inside), turn), slot, c, n0)
            store(made, final(g1, g2, g0, turn), slot, c, n1)

    copy_out(slot, s).start()

    @pl.when(s == 3)
    def _():
        copy_out(1 - slot, s - 1).wait()
        copy_out(slot, s).wait()


ROWS, COLS = 64, 256
PLANE = (ROWS, COLS)


def one(ref, s):
    return ref.at[pl.ds(s, 1)]


def whole(ref, s):
    return ref


def stream(ref, s):
    return ref


def flows(view):
    return view is stream or getattr(view, "streamed", False)


def pair(at, streamed=False):
    def view(ref, s):
        subject = pl.ds(0 if streamed else s, 1)
        if len(ref.shape) == 5:
            return ref.at[subject, :, pl.ds(at, 2)]
        return ref.at[subject, pl.ds(at, 2)]

    view.streamed = streamed
    return view


def call(kernel, info, ins, outs, scratch=(), us=1.0, mib=5):
    arrays, places = [], []
    streams = any(flows(view) for _, view in list(ins) + list(outs))
    for array, _ in ins:
        known = [i for i, other in enumerate(arrays) if other is array]
        if not known:
            arrays.append(array)
        places.append(known[0] if known else len(arrays) - 1)
    subjects = 4

    def body(info_ref, *refs):
        given, made = refs[: len(arrays)], refs[len(arrays) : len(arrays) + len(outs)]

        def per(s, _):
            views = [view(given[at], s) for at, (_, view) in zip(places, ins)]
            views += [view(ref, s) if view else ref for ref, (_, view) in zip(made, outs)]
            kernel(info_ref, s, *views, *refs[len(arrays) + len(outs) :])
            return 0

        if streams:
            per(pl.program_id(0), 0)
        else:
            lax.fori_loop(0, subjects, per, 0)

    vmem = pl.BlockSpec(memory_space=pltpu.VMEM)

    def block(dims):
        return pl.BlockSpec((1,) + dims[1:], lambda s: (s,) + (0,) * (len(dims) - 1))

    def made_of(dims, view):
        if view is stream:
            return block(dims), pltpu.HBM(dims, f32)
        if view is None:
            return pl.BlockSpec(memory_space=pl.ANY), pltpu.HBM(dims, f32)
        return vmem, jax.ShapeDtypeStruct(dims, f32)

    streamed = [any(flows(view) for other, view in ins if other is array) for array in arrays]
    operands = [pltpu.with_memory_space_constraint(a, pltpu.HBM) if st else a for a, st in zip(arrays, streamed)]
    out_specs, out_shapes = zip(*(made_of(*o) for o in outs))

    return pl.pallas_call(
        body,
        grid=(subjects,) if streams else (),
        in_specs=[pl.BlockSpec(memory_space=pltpu.SMEM)] + [block(a.shape) if st else vmem for a, st in zip(arrays, streamed)],
        out_specs=list(out_specs),
        out_shape=list(out_shapes),
        scratch_shapes=list(scratch),
        compiler_params=pltpu.CompilerParams(vmem_limit_bytes=mib * 1024 * 1024),
        cost_estimate=pl.CostEstimate(flops=0, bytes_accessed=int(us * 3.3e6), transcendentals=0),
        name=kernel.__name__,
    )(info, *operands)


def shards(template, momentum, targets, step_count):
    count = lax.axis_size("space")
    groups = lax.axis_size("subj")
    place = lax.axis_index("space")
    odd = place % 2
    core_pairs = [(i, i ^ 1) for i in range(count)]
    chip_pairs = [(i, ((i + 1) ^ 1) - 1) for i in range(1, count - 1)]

    def swap(array, role):
        return lax.ppermute(array, "space", (chip_pairs, core_pairs)[role])

    group = lax.axis_index("subj")
    inside = jnp.logical_and(place > 0, place < count - 1)
    info = jnp.concatenate([step_count, jnp.stack([odd, inside, group]).astype(jnp.int32)])

    def shape(*lead):
        return (step_count.shape[0],) + lead + PLANE

    def both(arrays, *views):
        return [(arrays[0], views[0]), (arrays[1], views[-1])]

    def near(array, streamed=False):
        return both((array, array), pair(0, streamed), pair(4, streamed))

    def out(*lead):
        return (shape(*lead), one)

    def out2(*lead):
        return [out(*lead)] * 2

    def planes(n):
        return pltpu.VMEM((n,) + PLANE, f32)

    def partner(array, by):
        return lax.ppermute(array, "subj", [(i, i ^ by) for i in range(groups)])

    ends = [lax.dynamic_slice_in_dim(momentum, at, 2, 2) for at in (6 * odd, 6 - 6 * odd)]
    across, ends = lax.optimization_barrier((partner(template, 1), ends))
    mr = [swap(ends[r], r) for r in ROLES]
    own, later = lax.optimization_barrier((jnp.stack([template, across]), momentum))
    rows = [own] + [partner(own, by) for by in (2, 4, 6)]
    w_in, w_edge, m_edge = call(
        velocity_inner, info, [(later, stream)], [out(3, 6), out(3, 2), out(3, 2)], us=5
    )
    rows, w_in, w_edge, m_edge = lax.optimization_barrier((rows, w_in, w_edge, m_edge))
    two_planes = ((2,) + PLANE, whole)
    t, dt, *t_sides = call(
        template_planes,
        info,
        [(x, whole) for x in rows],
        [((8,) + PLANE, whole), ((2, 8) + PLANE, whole), two_planes, two_planes],
        us=1,
    )
    tdt = [(t, whole), (dt, whole)]
    th = [swap(t_sides[r], r) for r in ROLES]
    slopes = pltpu.VMEM((2, 2) + PLANE, f32)
    i1_in, i2_in = call(inner_1, info, [(w_in, one)] + tdt, [out(6), out(4)], us=3)

    def side(r, *arrays):
        return [(x[r], one) if isinstance(x, (list, tuple)) else (x, pair((0, 4)[r])) for x in arrays]

    def sides(kernel, shared, arrays, *more, waits=None):
        made = [None, None]
        for r in (1, 0):
            made[r] = list(call(kernel(r), info, shared(r) + side(r, *arrays), *more))
            if r == 1 and waits is not None:
                arrays[waits][0], made[1][0] = lax.optimization_barrier((arrays[waits][0], made[1][0]))
        return [list(pair) for pair in zip(*made)]

    def exchange(pair):
        return [swap(pair[r], r) for r in ROLES]

    wb, i1b, s1 = [None, None], [None, None], [None, None]
    for r in (1, 0):
        given = [(m_edge, one), (w_edge, one)] + tdt + [(mr[r], stream), (th[r], whole)] + side(r, w_in, i1_in)
        wb[r], i1b[r], s1[r] = call(outer_1(r), info, given, [out(3, 2), out(2), out(2)], [slopes], 3)
        if r == 1:
            mr[0], s1[1] = lax.optimization_barrier((mr[0], s1[1]))
    r1 = exchange(s1)
    i3_in, i4_in, a4_in = call(
        inner_2,
        info,
        [(w_in, one), (i2_in, one)] + both(s1, one) + [(targets, one)],
        [out(6), out(4), out(4)],
        [planes(8)],
        us=4,
    )
    i3b, i4b, a4b, s2 = sides(
        outer_2, lambda r: [(targets, one)], [r1, wb, w_in, s1, i3_in], [out(2), out(2), out(1), out(2)], [], 2, waits=0
    )
    r2 = exchange(s2)
    a3_in, a2_in, g_in, warped = call(
        inner_3,
        info,
        [(w_in, one)]
        + both(wb, one)
        + both(s2, one)
        + both(a4b, one)
        + [(a4_in, one), (i3_in, one)]
        + both(i3b, one)
        + [(i2_in, one)]
        + both(s1, one)
        + [(i1_in, one), (i4_in, one)]
        + both(i4b, one),
        [out(6), out(4), out(3, 6), (shape(8), None)],
        [planes(8)] * 3 + [pltpu.SemaphoreType.DMA((8,))],
        us=7,
    )
    images = [i3b, i3_in, r1, s1, i1b, i1_in]
    a3b, a2b, s3 = sides(
        outer_3, lambda r: [], [r2, wb, w_in, s2, a3_in] + images, [out(2), out(2), out(3)], [], 2, waits=0
    )
    r3 = exchange(s3)
    small, six, tile = ((groups, n, 8, COLS) for n in (4, 6, 8))
    a1_in, total, g_full, *gb = call(
        inner_4,
        info,
        [(w_in, one)]
        + both(wb, one)
        + [(a2_in, one)]
        + both(a2b, one)
        + both(r2, one)
        + both(a3b, one)
        + both(s2, one)
        + both(s3, one)
        + both(i3b, one)
        + near(i3_in)
        + both(r1, one)
        + both(s1, one)
        + both(i1b, one)
        + near(i1_in)
        + tdt
        + [(g_in, one)],
        [out(6), (small, whole), out(3, 6)] + out2(3, 2),
        [planes(8)] * 2,
        us=5,
    )
    a1b = [None, None]
    for r in (1, 0):
        total, a1b[r] = call(
            outer_4(r),
            info,
            side(r, r3, wb, w_in, s3, a1_in) + [(total, whole)],
            [(six, whole) if r else (tile, None), (shape(2), None)],
            [pltpu.VMEM((groups, 2, 8, COLS), f32), pltpu.VMEM((4, 2) + PLANE, f32), pltpu.SemaphoreType.DMA((6,))],
            2,
        )
        if r == 1:
            r3[0], total = lax.optimization_barrier((r3[0], total))
    parts = lax.all_to_all(total, "subj", 0, 0)
    (momentum_gradient,) = call(
        finish,
        info,
        both(r3, stream) + both(a1b, stream) + both(gb, stream) + both(i1b, stream) + both(th, whole) + tdt + [(g_full, stream)],
        [(shape(3, 8), None)],
        [pltpu.VMEM((2, 3, 8) + PLANE, f32), pltpu.SemaphoreType.DMA((2,)), slopes],
        us=6,
        mib=14,
    )
    template_gradient = jnp.sum(parts, axis=0)
    return (warped, template_gradient, momentum_gradient)


def solution(mesh):
    in_specs = (
        P("space", "subj", None),
        P("subj", None, "space", None, None),
        P("subj", "space", None, None),
        P("subj"),
    )
    out_specs = (
        P("subj", "space", None, None),
        P("space", "subj", None),
        P("subj", None, "space", None, None),
    )
    return jax.shard_map(shards, mesh=mesh, in_specs=in_specs, out_specs=out_specs, check_vma=False)
```

```python
import jax
import jax.numpy as jnp
from jax import lax
from jax.experimental import pallas as pl
from jax.experimental.pallas import tpu as pltpu
from jax.sharding import PartitionSpec as P

time_step = 0.15
smoothing = 0.1
half = 0.5 * time_step
centre = 1.0 - 6.0 * smoothing
f32 = jnp.float32


class Plane:
    def __init__(self, rows):
        self.rows, self.known, self.rolled = rows, {}, {}

    def at(self, b):
        if b not in self.known:
            self.known[b] = tuple(self.rows(b))
        return self.known[b]

    def turned(self, b, by):
        if (b, by) not in self.rolled:
            self.rolled[b, by] = tuple(pltpu.roll(x, by, axis=0) for x in self.at(b))
        return self.rolled[b, by]


BLOCKS = 8


def halves(h):
    return pl.ds(128 * h, 128)


def load(ref, *at):
    return Plane(lambda b: [ref[at + (pl.ds(8 * b, 8), halves(h))] for h in (0, 1)])


def store(ref, plane, *at):
    store_all([(ref, plane, at)])


def store_all(targets):
    for b in range(BLOCKS):
        for ref, plane, at in targets:
            for h, value in enumerate(plane.at(b)):
                ref[at + (pl.ds(8 * b, 8), halves(h))] = value


def add_t(ref, plane, p):
    for b in range(BLOCKS):
        for h, value in enumerate(plane.at(b)):
            ref[b, p, :, halves(h)] += value


def each(fn, *planes):
    return Plane(lambda b: [fn(*x) for x in zip(*(plane.at(b) for plane in planes))])


def add(*planes):
    total = planes[0]
    for plane in planes[1:]:
        total = each(lambda a, b: a + b, total, plane)
    return total


def sub(a, b):
    return each(lambda x, y: x - y, a, b)


def mul(a, b):
    return each(lambda x, y: x * y, a, b)


def scale(a, factor):
    return each(lambda x: x * factor, a)


def y_sides(plane):
    def rows(b, by, edge, step):
        row = lax.broadcasted_iota(jnp.int32, (8, 128), 0)
        here, there = plane.turned(b, by), b + step
        over = plane.turned(there, by) if 0 <= there < BLOCKS else (0.0, 0.0)
        return [jnp.where(row == edge, o, x) for o, x in zip(over, here)]

    return Plane(lambda b: rows(b, 1, 0, -1)), Plane(lambda b: rows(b, 7, 7, 1))


def x_sides(plane):
    def before(b):
        lane = lax.broadcasted_iota(jnp.int32, (8, 128), 1)
        left, right = (pltpu.roll(x, 1, axis=1) for x in plane.at(b))
        return jnp.where(lane == 0, 0.0, left), jnp.where(lane == 0, left, right)

    def after(b):
        lane = lax.broadcasted_iota(jnp.int32, (8, 128), 1)
        left, right = (pltpu.roll(x, 127, axis=1) for x in plane.at(b))
        return jnp.where(lane == 127, right, left), jnp.where(lane == 127, 0.0, right)

    return Plane(before), Plane(after)


def dy(plane):
    before, after = y_sides(plane)
    return sub(after, before)


def dx(plane):
    before, after = x_sides(plane)
    return sub(after, before)


def smooth(mid, inner, outer, a, b):
    total = add(*(plane for plane in (inner, outer) if plane is not None), *y_sides(mid), *x_sides(mid))
    return each(lambda m, t: a * m + b * t, mid, total)


def dz(inner, outer, toward):
    return sub(inner, outer) if toward > 0 else sub(outer, inner)


def forward(mid, inner, outer, w, toward=1):
    change = add(mul(w[0], dz(inner, outer, toward)), mul(w[1], dy(mid)), mul(w[2], dx(mid)))
    return sub(mid, change)


def forward_by(mid, inner, outer, slopes, w, toward=1):
    change = add(mul(w[0], dz(inner, outer, toward)), mul(w[1], slopes[0]), mul(w[2], slopes[1]))
    return sub(mid, change)


def backward(mid, flux_inner, flux_outer, wy, wx, toward=1, active=None):
    change = add(dz(flux_inner, flux_outer, toward), dy(mul(wy, mid)), dx(mul(wx, mid)))
    return add(mid, change if active is None else scale(change, active))


def grads(adj, mid, inner, outer, toward=1, slopes=None):
    sy, sx = slopes or (dy(mid), dx(mid))
    return [mul(adj, dz(inner, outer, toward)), mul(adj, sy), mul(adj, sx)]


def natural(odd, j):
    return j + odd * (7 - 2 * j)


def unrolled(low, high, step):
    for j in range(low, high):
        step(j, 0)


ROLES = (0, 1)
TOWARD = (1, -1)


def t_load(t, k, role=0):
    return load(t, k if role == 0 else 7 - k)


def t_slopes(dt, k, role=0):
    return [load(dt, c, k if role == 0 else 7 - k) for c in (0, 1)]


def named(kernel, name, role):
    kernel.__name__ = name + ("_chip", "_core")[role]
    return kernel


def halo_slopes(s, th, slopes, roles=ROLES):
    @pl.when(s == 0)
    def _():
        for r in roles:
            mid = load(th[r], 0)
            store_all([(slopes, dy(mid), (r, 0)), (slopes, dx(mid), (r, 1))])

    return {r: [load(slopes, r, c) for c in (0, 1)] for r in roles}


def template_planes(info, s, *refs):
    *sources, t, dt, send_z, send_c = refs
    odd, me = info[4], info[6]

    @pl.when(s == 0)
    def _():
        for j in range(8):
            for i, source in enumerate(sources):
                for x in (0, 1):
                    row = pl.multiple_of(8 * jnp.bitwise_xor(me, 2 * i + x), 8)
                    t[j, pl.ds(row, 8)] = source[x, natural(odd, j)]
        for i in (0, 1):
            send_z[i] = t[i]
            send_c[i] = t[7 - i]
        for j in range(8):
            mid = load(t, j)
            store_all([(dt, dy(mid), (0, j)), (dt, dx(mid), (1, j))])


def momentum_ends(info, s, m, chip, core, sems):
    odd = info[4]
    copies = [
        pltpu.make_async_copy(m.at[at, :, pl.ds(first, 2)], end.at[at], sems.at[at, i])
        for i, (end, first) in enumerate(((chip, 6 * odd), (core, 6 - 6 * odd)))
        for at in range(4)
    ]

    @pl.when(s == 0)
    def _():
        for copy in copies:
            copy.start()
        for copy in copies:
            copy.wait()


def velocity_inner(info, s, m, w_in, w_edge, m_edge):
    odd = info[4]
    sign = (1 - 2 * odd).astype(f32)
    for j in range(8):
        for c in range(3):
            turn = sign if c == 0 else 1.0
            v = smooth(
                load(m, 0, c, natural(odd, j)),
                load(m, 0, c, natural(odd, j + 1)) if j < 7 else None,
                load(m, 0, c, natural(odd, j - 1)) if j > 0 else None,
                half * centre * turn,
                half * smoothing * turn,
            )
            if 0 < j < 7:
                store(w_in, v, 0, c, j - 1)
            else:
                store(w_edge, v, 0, c, j // 7)
                m_edge[0, c, j // 7] = m[0, c, natural(odd, j)]


def inner_1(info, s, w_in, t, dt, i1_in, i2_in):
    def first(j, _):
        w = [load(w_in, 0, c, j - 1) for c in range(3)]
        image = forward_by(t_load(t, j), t_load(t, j + 1), t_load(t, j - 1), t_slopes(dt, j), w)
        store(i1_in, image, 0, j - 1)
        return 0

    unrolled(1, 7, first)

    @pl.when(info[s] > 1)
    def _():
        def second(j, _):
            at = lambda i: load(i1_in, 0, i - 1)
            w = [load(w_in, 0, c, j - 1) for c in range(3)]
            store(i2_in, forward(at(j), at(j + 1), at(j - 1), w), 0, j - 2)
            return 0

        unrolled(2, 6, second)

    @pl.when(info[s] <= 1)
    def _():
        i2_in[0] = i1_in[0, 1:5]


def outer_1(role):
    roles = (role,)

    def kernel(info, s, *refs):
        m_edge, w_edge, t, dt = refs[:4]
        mr, th, wp, i1p, w_out, i1_out, send = ({role: ref} for ref in refs[4:11])
        slopes = halo_slopes(s, th, refs[11], roles)
        odd = info[4]
        sign = (1 - 2 * odd).astype(f32)
        for r in roles:
            to = TOWARD[r]
            h1 = 1 - odd if r == 0 else odd
            inside = info[5].astype(f32) if r == 0 else 1.0
            wh, w0 = [], []
            for c in range(3):
                turn = sign if c == 0 else 1.0
                m_h1, m_p0 = load(mr[r], 0, c, h1), load(m_edge, 0, c, r)
                a, b = half * centre * turn, half * smoothing * turn
                wh.append(smooth(m_h1, m_p0, load(mr[r], 0, c, 1 - h1), a * inside, b * inside))
                w0.append(add(load(w_edge, 0, c, r), scale(m_h1, b)))
            th1, th2, tp0, tp1 = load(th[r], 0), load(th[r], 1), t_load(t, 0, r), t_load(t, 1, r)
            i_h1 = forward_by(th1, tp0, th2, slopes[r], wh, to)
            i_p0 = forward_by(tp0, tp1, th1, t_slopes(dt, 0, r), w0, to)
            targets = [(i1_out[r], i_h1, (0, 0)), (i1_out[r], i_p0, (0, 1))]
            targets += [(w_out[r], w[c], (0, c, i)) for i, w in enumerate((wh, w0)) for c in range(3)]
            store_all(targets)

        @pl.when(info[s] > 1)
        def _():
            for r in roles:
                to, near, far = TOWARD[r], r, 1 - r
                i_h1, i_p0 = load(i1_out[r], 0, 0), load(i1_out[r], 0, 1)
                i_p1, i_p2 = load(i1p[r], 0, near), load(i1p[r], 0, far)
                w0 = [load(w_out[r], 0, c, 1) for c in range(3)]
                w1 = [load(wp[r], 0, c, near) for c in range(3)]
                store(send[r], forward(i_p0, i_p1, i_h1, w0, to), 0, 0)
                store(send[r], forward(i_p1, i_p2, i_p0, w1, to), 0, 1)

        @pl.when(info[s] <= 1)
        def _():
            for r in roles:
                send[r][0, 0] = i1_out[r][0, 1]
                send[r][0, 1] = i1p[r][0, r]

    return named(kernel, "outer_1", role)


def gather_planes(x, sides, inner):
    x[0] = sides[0][0, 0]
    x[1] = sides[0][0, 1]
    x[7] = sides[1][0, 0]
    x[6] = sides[1][0, 1]
    x[2:6] = inner[0]


def inner_2(info, s, w_in, i2_in, s1z, s1c, targets, i3_in, i4_in, a4_in, x):
    odd = info[4]
    gather_planes(x, (s1z, s1c), i2_in)

    @pl.when(info[s] > 2)
    def _():
        def step(j, _):
            w = [load(w_in, 0, c, j - 1) for c in range(3)]
            store(i3_in, forward(load(x, j), load(x, j + 1), load(x, j - 1), w), 0, j - 1)
            return 0

        unrolled(1, 7, step)

    @pl.when(info[s] <= 2)
    def _():
        i3_in[0] = x[1:7]

    @pl.when(info[s] > 3)
    def _():
        def step(j, _):
            at = lambda i: load(i3_in, 0, i - 1)
            w = [load(w_in, 0, c, j - 1) for c in range(3)]
            image = forward(at(j), at(j + 1), at(j - 1), w)
            late = sub(image, load(targets, 0, natural(odd, j)))
            store_all([(i4_in, image, (0, j - 2)), (a4_in, late, (0, j - 2))])
            return 0

        unrolled(2, 6, step)

    @pl.when(info[s] <= 3)
    def _():
        def step(j, _):
            image = load(i3_in, 0, j - 1)
            late = sub(image, load(targets, 0, natural(odd, j)))
            store_all([(i4_in, image, (0, j - 2)), (a4_in, late, (0, j - 2))])
            return 0

        unrolled(2, 6, step)


def outer_2(role):
    roles = (role,)

    def kernel(info, s, *refs):
        targets = refs[0]
        r1, wb, wp, s1, i3p, i3_out, i4_out, a4_out, send = ({role: ref} for ref in refs[1:])
        odd = info[4]

        @pl.when(info[s] > 2)
        def _():
            for r in roles:
                i_h1, i_h2 = load(r1[r], 0, 0), load(r1[r], 0, 1)
                i_p0, i_p1 = load(s1[r], 0, 0), load(s1[r], 0, 1)
                wh = [load(wb[r], 0, c, 0) for c in range(3)]
                w0 = [load(wb[r], 0, c, 1) for c in range(3)]
                store(i3_out[r], forward(i_h1, i_p0, i_h2, wh, TOWARD[r]), 0, 0)
                store(i3_out[r], forward(i_p0, i_p1, i_h1, w0, TOWARD[r]), 0, 1)

        @pl.when(info[s] <= 2)
        def _():
            for r in roles:
                i3_out[r][0, 0] = r1[r][0, 0]
                i3_out[r][0, 1] = s1[r][0, 0]

        def late(r, i4_p0, i4_p1):
            n = [natural(odd, k if r == 0 else 7 - k) for k in (0, 1)]
            a_p0, a_p1 = sub(i4_p0, load(targets, 0, n[0])), sub(i4_p1, load(targets, 0, n[1]))
            store_all([(i4_out[r], i4_p0, (0, 0)), (send[r], a_p0, (0, 0))])
            f_p1 = mul(load(wp[r], 0, 0, r), a_p1)
            store_all([(i4_out[r], i4_p1, (0, 1)), (a4_out[r], a_p1, (0, 0)), (send[r], f_p1, (0, 1))])

        @pl.when(info[s] > 3)
        def _():
            for r in roles:
                to, near, far = TOWARD[r], r, 1 - r
                i_h1, i_p0 = load(i3_out[r], 0, 0), load(i3_out[r], 0, 1)
                i_p1, i_p2 = load(i3p[r], 0, near), load(i3p[r], 0, far)
                w0 = [load(wb[r], 0, c, 1) for c in range(3)]
                w1 = [load(wp[r], 0, c, near) for c in range(3)]
                late(r, forward(i_p0, i_p1, i_h1, w0, to), forward(i_p1, i_p2, i_p0, w1, to))

        @pl.when(info[s] <= 3)
        def _():
            for r in roles:
                late(r, load(i3_out[r], 0, 1), load(i3p[r], 0, r))

    return named(kernel, "outer_2", role)


def inner_3(info, s, *refs):
    w_in, wbz, wbc, s2z, s2c, a4z, a4c, a4_in, i3_in, i3z, i3c, i2_in, s1z, s1c, i1_in, i4_in, i4z, i4c = refs[:18]
    a3_in, a2_in, g_in, warped, a, f, x, sems = refs[18:]
    odd = info[4]

    def copies():
        def one(source, j):
            return pltpu.make_async_copy(source, warped.at[s, natural(odd, j)], sems.at[j])

        pairs = [(i4z.at[0, 0], 0), (i4z.at[0, 1], 1), (i4c.at[0, 1], 6), (i4c.at[0, 0], 7)]
        pairs += [(i4_in.at[0, j - 2], j) for j in range(2, 6)]
        return [one(source, j) for source, j in pairs]

    for copy in copies():
        copy.start()
    a[0], a[7] = s2z[0, 0], s2c[0, 0]
    a[1], a[6] = a4z[0, 0], a4c[0, 0]
    a[2:6] = a4_in[0]

    @pl.when(info[s] > 3)
    def _():
        x[0], x[7] = i3z[0, 1], i3c[0, 1]
        x[1:7] = i3_in[0]
        f[0] = wbz[0, 0, 1] * a[0]
        f[7] = wbc[0, 0, 1] * a[7]
        f[1:7] = w_in[0, 0] * a[1:7]

        def step(j, _):
            mid = load(a, j)
            wy, wx = (load(w_in, 0, c, j - 1) for c in (1, 2))
            adj = backward(mid, load(f, j + 1), load(f, j - 1), wy, wx)
            g = grads(mid, load(x, j), load(x, j + 1), load(x, j - 1))
            store_all([(a3_in, adj, (0, j - 1))] + [(g_in, g[c], (0, c, j - 1)) for c in range(3)])
            return 0

        unrolled(1, 7, step)

    @pl.when(info[s] <= 3)
    def _():
        a3_in[0] = a[1:7]
        g_in[...] = jnp.zeros(g_in.shape, f32)

    @pl.when(info[s] > 2)
    def _():
        gather_planes(x, (s1z, s1c), i2_in)
        f[1:7] = w_in[0, 0] * a3_in[0]

        def gradient(j, adj):
            g = grads(adj, load(x, j), load(x, j + 1), load(x, j - 1))
            return [(g_in, add(load(g_in, 0, c, j - 1), g[c]), (0, c, j - 1)) for c in range(3)]

        def end(i, _):
            j = 1 + 5 * i
            store_all(gradient(j, load(a3_in, 0, j - 1)))
            return 0

        unrolled(0, 2, end)

        def step(j, _):
            mid = load(a3_in, 0, j - 1)
            wy, wx = (load(w_in, 0, c, j - 1) for c in (1, 2))
            adj = backward(mid, load(f, j + 1), load(f, j - 1), wy, wx)
            store_all([(a2_in, adj, (0, j - 2))] + gradient(j, mid))
            return 0

        unrolled(2, 6, step)

    @pl.when(info[s] <= 2)
    def _():
        a2_in[0] = a3_in[0, 1:5]

    @pl.when(info[s] > 1)
    def _():
        def step(j, _):
            at = lambda i: load(i1_in, 0, i - 1)
            g = grads(load(a2_in, 0, j - 2), at(j), at(j + 1), at(j - 1))
            store_all([(g_in, add(load(g_in, 0, c, j - 1), g[c]), (0, c, j - 1)) for c in range(3)])
            return 0

        unrolled(2, 6, step)

    for copy in copies():
        copy.wait()


def outer_3(role):
    roles = (role,)

    def kernel(info, s, *refs):
        r2, wb, wp, s2, a3p, i3b, i3p, r1, s1, i1b, i1p, a3, a2_out, send = ({role: ref} for ref in refs)

        def gz(r, adj, inner, outer):
            return (send[r], add(load(send[r], 0, 2), mul(adj, dz(inner, outer, TOWARD[r]))), (0, 2))


        @pl.when(info[s] > 3)
        def _():
            for r in roles:
                to = TOWARD[r]
                a_h1, a_p0 = load(r2[r], 0, 0), load(s2[r], 0, 0)
                f_h2, f_p1 = scale(load(r2[r], 0, 1), -1.0), load(s2[r], 0, 1)
                wh = [load(wb[r], 0, c, 0) for c in range(3)]
                w0 = [load(wb[r], 0, c, 1) for c in range(3)]
                store(a3[r], backward(a_h1, mul(w0[0], a_p0), f_h2, wh[1], wh[2], to), 0, 0)
                b_p0 = backward(a_p0, f_p1, mul(wh[0], a_h1), w0[1], w0[2], to)
                g = mul(a_p0, dz(load(i3p[r], 0, r), load(i3b[r], 0, 0), to))
                store_all([(a3[r], b_p0, (0, 1)), (send[r], g, (0, 2))])

        @pl.when(info[s] <= 3)
        def _():
            for r in roles:
                a3[r][0, 0] = r2[r][0, 0]
                a3[r][0, 1] = s2[r][0, 0]
                send[r][0, 2] = jnp.zeros(send[r].shape[2:], f32)

        def late(r, a2_p0, a2_p1):
            f_p1 = mul(load(wp[r], 0, 0, r), a2_p1)
            store_all([(a2_out[r], a2_p0, (0, 0)), (send[r], a2_p0, (0, 0))])
            store_all([(a2_out[r], a2_p1, (0, 1)), (send[r], f_p1, (0, 1))])

        @pl.when(info[s] > 2)
        def _():
            for r in roles:
                to, near, far = TOWARD[r], r, 1 - r
                a_h1, a_p0 = load(a3[r], 0, 0), load(a3[r], 0, 1)
                a_p1, a_p2 = load(a3p[r], 0, near), load(a3p[r], 0, far)
                wh0 = load(wb[r], 0, 0, 0)
                w0 = [load(wb[r], 0, c, 1) for c in range(3)]
                w1 = [load(wp[r], 0, c, near) for c in range(3)]
                f_p2 = mul(load(wp[r], 0, 0, far), a_p2)
                store_all([gz(r, a_p0, load(s1[r], 0, 1), load(r1[r], 0, 0))])
                late(
                    r,
                    backward(a_p0, mul(w1[0], a_p1), mul(wh0, a_h1), w0[1], w0[2], to),
                    backward(a_p1, f_p2, mul(w0[0], a_p0), w1[1], w1[2], to),
                )

        @pl.when(info[s] <= 2)
        def _():
            for r in roles:
                late(r, load(a3[r], 0, 1), load(a3p[r], 0, r))

        @pl.when(info[s] > 1)
        def _():
            for r in roles:
                store_all([gz(r, load(a2_out[r], 0, 0), load(i1p[r], 0, r), load(i1b[r], 0, 0))])

    return named(kernel, "outer_3", role)


def inner_4(info, s, *refs):
    w_in, wbz, wbc, a2_in, a2z, a2c, *rest, a1_in, total, g_full, gbz, gbc, a, f = refs
    gather_planes(a, (a2z, a2c), a2_in)

    @pl.when(s == 0)
    def _():
        total[...] = jnp.zeros(total.shape, f32)

    @pl.when(info[s] > 1)
    def _():
        f[0] = wbz[0, 0, 1] * a[0]
        f[7] = wbc[0, 0, 1] * a[7]
        f[1:7] = w_in[0, 0] * a[1:7]

        def step(j, _):
            mid = load(a, j)
            wy, wx = (load(w_in, 0, c, j - 1) for c in (1, 2))
            store(a1_in, backward(mid, load(f, j + 1), load(f, j - 1), wy, wx), 0, j - 1)
            return 0

        unrolled(1, 7, step)

    @pl.when(info[s] <= 1)
    def _():
        a1_in[0] = a[1:7]

    f[1:7] = w_in[0, 0] * a1_in[0]

    def last(j, _):
        mid = load(a1_in, 0, j - 1)
        wy, wx = (load(w_in, 0, c, j - 1) for c in (1, 2))
        adj = backward(mid, load(f, j + 1), load(f, j - 1), wy, wx)
        add_t(total, adj, j - 2)
        return 0

    unrolled(2, 6, last)
    r2, a3, s2, s3, i3b, i3p, r1, s1, i1b, i1p = (rest[2 * i : 2 * i + 2] for i in range(10))
    t, dt, g_in = rest[20:23]
    a2b, gb = (a2z, a2c), (gbz, gbc)

    def step(j, _):
        adj = load(a1_in, 0, j - 1)
        g = grads(adj, None, t_load(t, j + 1), t_load(t, j - 1), slopes=t_slopes(dt, j))
        store_all([(g_full, add(load(g_in, 0, c, j - 1), g[c]), (0, c, j - 1)) for c in range(3)])
        return 0

    unrolled(1, 7, step)
    for r in ROLES:
        to, near, far = TOWARD[r], r, 1 - r
        p1 = 0 if r == 0 else 5
        g = gb[r]

        def more(plane, parts, first=False):
            values = [(g, value if first else add(load(g, 0, c, plane), value), (0, c, plane)) for c, value in parts]
            store_all(values)

        def at_h1(adj, image):
            return [(1, mul(adj, dy(image))), (2, mul(adj, dx(image)))]

        def at_p0(adj, *images):
            return list(enumerate(grads(adj, *images, to)))[1:]

        @pl.when(info[s] > 3)
        def _():
            i_h1, i_p0 = load(i3b[r], 0, 0), load(i3b[r], 0, 1)
            more(0, at_h1(load(r2[r], 0, 0), i_h1), True)
            more(1, at_p0(load(s2[r], 0, 0), i_p0, load(i3p[r], 0, near), i_h1), True)

        @pl.when(info[s] <= 3)
        def _():
            g[...] = jnp.zeros(g.shape, f32)

        @pl.when(info[s] > 2)
        def _():
            i_h1, i_p0 = load(r1[r], 0, 0), load(s1[r], 0, 0)
            more(0, at_h1(load(a3[r], 0, 0), i_h1))
            more(1, at_p0(load(a3[r], 0, 1), i_p0, load(s1[r], 0, 1), i_h1))

        @pl.when(info[s] > 1)
        def _():
            i_h1, i_p0 = load(i1b[r], 0, 0), load(i1b[r], 0, 1)
            i_p1, i_p2 = load(i1p[r], 0, near), load(i1p[r], 0, far)
            more(1, at_p0(load(a2b[r], 0, 0), i_p0, i_p1, i_h1))
            g1 = grads(load(a2b[r], 0, 1), i_p1, i_p2, i_p0, to)
            store_all([(g_full, add(load(g_full, 0, c, p1), g1[c]), (0, c, p1)) for c in range(3)])

        g[0, 0, 1] = s3[r][0, 2]


def outer_4(role):
    to, near, far = TOWARD[role], role, 1 - role

    def kernel(info, s, *refs):
        r3, wb, wp, s3, a1p, total_in, total_out, a1_out = refs[:8]
        total, a1s, sems = refs[8:]
        odd = info[4]
        first = 2 - 2 * odd

        def sent(at):
            return pltpu.make_async_copy(a1s.at[at], a1_out.at[at], sems.at[at])

        def six():
            return pltpu.make_async_copy(total_in, total_out.at[:, pl.ds(first, 6)], sems.at[4])

        @pl.when(s == 0)
        def _():
            if role == 0:
                six().start()
                total[...] = jnp.zeros(total.shape, f32)
            else:
                for j in range(2, 6):
                    total_out[:, natural(odd, j) - first] = total_in[:, j - 2]
                for j in (6, 7):
                    total_out[:, natural(odd, j) - first] = jnp.zeros((8, 8, COLS), f32)

        active = (info[s] > 1).astype(f32)
        a_h1, a_p0 = load(r3, 0, 0), load(s3, 0, 0)
        f_h2, f_p1 = scale(load(r3, 0, 1), -1.0), load(s3, 0, 1)
        wh = [load(wb, 0, c, 0) for c in range(3)]
        w0 = [load(wb, 0, c, 1) for c in range(3)]
        b_h1 = backward(a_h1, mul(w0[0], a_p0), f_h2, wh[1], wh[2], to, active)
        b_p0 = backward(a_p0, f_p1, mul(wh[0], a_h1), w0[1], w0[2], to, active)
        store_all([(a1s, b_h1, (s, 0)), (a1s, b_p0, (s, 1))])
        sent(s).start()
        w1 = [load(wp, 0, c, near) for c in range(3)]
        b_p1, b_p2 = load(a1p, 0, near), load(a1p, 0, far)
        c_p0 = backward(b_p0, mul(w1[0], b_p1), mul(wh[0], b_h1), w0[1], w0[2], to)
        c_p1 = backward(b_p1, mul(load(wp, 0, 0, far), b_p2), mul(w0[0], b_p0), w1[1], w1[2], to)
        for k, value in enumerate((c_p0, c_p1)):
            if role == 0:
                add_t(total, value, natural(odd, k) - 6 * odd)
            else:
                add_t(total_out, value, natural(odd, 7 - k) - first)

        @pl.when(s == 3)
        def _():
            if role == 0:
                last = pltpu.make_async_copy(total, total_out.at[:, pl.ds(6 * odd, 2)], sems.at[5])
                last.start()
                last.wait()
                six().wait()
            for at in range(4):
                sent(at).wait()

    return named(kernel, "outer_4", role)


def final(mid, inner, outer, turn):
    return smooth(mid, inner, outer, -half * centre * turn, -half * smoothing * turn)


def finish(info, s, *refs):
    r3, a1b, gb, i1b = (refs[2 * i : 2 * i + 2] for i in range(4))
    th, (t, dt, g_full, mg, made, sems, halo) = refs[8:10], refs[10:]
    slopes_h1 = halo_slopes(s, th, halo)
    odd = info[4]
    sign = (1 - 2 * odd).astype(f32)
    slot = lax.rem(s, 2)

    def copy_out(which, at):
        return pltpu.make_async_copy(made.at[which], mg.at[at], sems.at[which])

    @pl.when(s >= 2)
    def _():
        copy_out(slot, s - 2).wait()

    def step(j, _):
        for c in range(3):
            at = lambda i: load(g_full, 0, c, i - 1)
            store(made, final(at(j), at(j + 1), at(j - 1), sign if c == 0 else 1.0), slot, c, natural(odd, j))
        return 0

    unrolled(2, 6, step)
    for r in ROLES:
        to = TOWARD[r]
        p1, p2 = (0, 1) if r == 0 else (5, 4)
        n0, n1 = (natural(odd, k if r == 0 else 7 - k) for k in (0, 1))
        inside = info[5].astype(f32) if r == 0 else 1.0
        step_one = (info[s] > 1).astype(f32)
        th1, th2, tp0, tp1 = load(th[r], 0), load(th[r], 1), t_load(t, 0, r), t_load(t, 1, r)
        slopes = slopes_h1[r]
        a_one = scale(load(r3[r], 0, 0), step_one)
        i_h1 = load(i1b[r], 0, 0)
        b_h1, b_p0 = load(a1b[r], 0, 0), load(a1b[r], 0, 1)
        g_h1 = [
            add(scale(load(r3[r], 0, 2), -1.0), mul(b_h1, dz(tp0, th2, to))),
            add(load(gb[r], 0, 1, 0), mul(a_one, dy(i_h1)), mul(b_h1, slopes[0])),
            add(load(gb[r], 0, 2, 0), mul(a_one, dx(i_h1)), mul(b_h1, slopes[1])),
        ]
        g_p0 = grads(b_p0, tp0, tp1, th1, to, t_slopes(dt, 0, r))
        for c in range(3):
            turn = sign if c == 0 else 1.0
            g0 = add(load(gb[r], 0, c, 1), g_p0[c])
            g1, g2 = load(g_full, 0, c, p1), load(g_full, 0, c, p2)
            store(made, final(g0, g1, scale(g_h1[c], inside), turn), slot, c, n0)
            store(made, final(g1, g2, g0, turn), slot, c, n1)

    copy_out(slot, s).start()

    @pl.when(s == 3)
    def _():
        copy_out(1 - slot, s - 1).wait()
        copy_out(slot, s).wait()


ROWS, COLS = 64, 256
PLANE = (ROWS, COLS)


def one(ref, s):
    return ref.at[pl.ds(s, 1)]


def whole(ref, s):
    return ref


def stream(ref, s):
    return ref


def far_off(ref, s):
    return ref


def flows(view):
    return view is stream or getattr(view, "streamed", False)


def pair(at, streamed=False):
    def view(ref, s):
        subject = pl.ds(0 if streamed else s, 1)
        if len(ref.shape) == 5:
            return ref.at[subject, :, pl.ds(at, 2)]
        return ref.at[subject, pl.ds(at, 2)]

    view.streamed = streamed
    return view


def call(kernel, info, ins, outs, scratch=(), us=1.0, mib=5):
    arrays, places = [], []
    streams = any(flows(view) for _, view in list(ins) + list(outs))
    for array, _ in ins:
        known = [i for i, other in enumerate(arrays) if other is array]
        if not known:
            arrays.append(array)
        places.append(known[0] if known else len(arrays) - 1)
    subjects = 4

    def body(info_ref, *refs):
        given, made = refs[: len(arrays)], refs[len(arrays) : len(arrays) + len(outs)]

        def per(s, _):
            views = [view(given[at], s) for at, (_, view) in zip(places, ins)]
            views += [view(ref, s) if view else ref for ref, (_, view) in zip(made, outs)]
            kernel(info_ref, s, *views, *refs[len(arrays) + len(outs) :])
            return 0

        if streams:
            per(pl.program_id(0), 0)
        else:
            lax.fori_loop(0, subjects, per, 0)

    vmem = pl.BlockSpec(memory_space=pltpu.VMEM)

    def block(dims):
        return pl.BlockSpec((1,) + dims[1:], lambda s: (s,) + (0,) * (len(dims) - 1))

    def made_of(dims, view):
        if view is stream:
            return block(dims), pltpu.HBM(dims, f32)
        if view is None:
            return pl.BlockSpec(memory_space=pl.ANY), pltpu.HBM(dims, f32)
        return vmem, jax.ShapeDtypeStruct(dims, f32)

    streamed = [any(flows(view) for other, view in ins if other is array) for array in arrays]
    remote = [any(view is far_off for other, view in ins if other is array) for array in arrays]
    operands = [
        pltpu.with_memory_space_constraint(a, pltpu.HBM) if st or re else a for a, st, re in zip(arrays, streamed, remote)
    ]
    out_specs, out_shapes = zip(*(made_of(*o) for o in outs))

    return pl.pallas_call(
        body,
        grid=(subjects,) if streams else (),
        in_specs=[pl.BlockSpec(memory_space=pltpu.SMEM)] + [
            pl.BlockSpec(memory_space=pl.ANY) if re else block(a.shape) if st else vmem
            for a, st, re in zip(arrays, streamed, remote)
        ],
        out_specs=list(out_specs),
        out_shape=list(out_shapes),
        scratch_shapes=list(scratch),
        compiler_params=pltpu.CompilerParams(vmem_limit_bytes=mib * 1024 * 1024),
        cost_estimate=pl.CostEstimate(flops=0, bytes_accessed=int(us * 3.3e6), transcendentals=0),
        name=kernel.__name__,
    )(info, *operands)


def shards(template, momentum, targets, step_count):
    count = lax.axis_size("space")
    groups = lax.axis_size("subj")
    place = lax.axis_index("space")
    odd = place % 2
    core_pairs = [(i, i ^ 1) for i in range(count)]
    chip_pairs = [(i, ((i + 1) ^ 1) - 1) for i in range(1, count - 1)]

    def swap(array, role):
        return lax.ppermute(array, "space", (chip_pairs, core_pairs)[role])

    group = lax.axis_index("subj")
    inside = jnp.logical_and(place > 0, place < count - 1)
    info = jnp.concatenate([step_count, jnp.stack([odd, inside, group]).astype(jnp.int32)])

    def shape(*lead):
        return (step_count.shape[0],) + lead + PLANE

    def both(arrays, *views):
        return [(arrays[0], views[0]), (arrays[1], views[-1])]

    def near(array, streamed=False):
        return both((array, array), pair(0, streamed), pair(4, streamed))

    def out(*lead):
        return (shape(*lead), one)

    def out2(*lead):
        return [out(*lead)] * 2

    def planes(n):
        return pltpu.VMEM((n,) + PLANE, f32)

    def partner(array, by):
        return lax.ppermute(array, "subj", [(i, i ^ by) for i in range(groups)])

    ends = call(
        momentum_ends,
        info,
        [(momentum, far_off)],
        [(shape(3, 2), whole), (shape(3, 2), whole)],
        [pltpu.SemaphoreType.DMA((4, 2))],
    )
    across, ends = lax.optimization_barrier((partner(template, 1), ends))
    mr = [swap(ends[r], r) for r in ROLES]
    own, later = lax.optimization_barrier((jnp.stack([template, across]), momentum))
    rows = [own] + [partner(own, by) for by in (2, 4, 6)]
    w_in, w_edge, m_edge = call(
        velocity_inner, info, [(later, stream)], [out(3, 6), out(3, 2), out(3, 2)], us=5
    )
    rows, w_in, w_edge, m_edge = lax.optimization_barrier((rows, w_in, w_edge, m_edge))
    two_planes = ((2,) + PLANE, whole)
    t, dt, *t_sides = call(
        template_planes,
        info,
        [(x, whole) for x in rows],
        [((8,) + PLANE, whole), ((2, 8) + PLANE, whole), two_planes, two_planes],
        us=1,
    )
    tdt = [(t, whole), (dt, whole)]
    th = [swap(t_sides[r], r) for r in ROLES]
    slopes = pltpu.VMEM((2, 2) + PLANE, f32)
    i1_in, i2_in = call(inner_1, info, [(w_in, one)] + tdt, [out(6), out(4)], us=3)

    def side(r, *arrays):
        return [(x[r], one) if isinstance(x, (list, tuple)) else (x, pair((0, 4)[r])) for x in arrays]

    def sides(kernel, shared, arrays, *more, waits=None):
        made = [None, None]
        for r in (1, 0):
            made[r] = list(call(kernel(r), info, shared(r) + side(r, *arrays), *more))
            if r == 1 and waits is not None:
                arrays[waits][0], made[1][0] = lax.optimization_barrier((arrays[waits][0], made[1][0]))
        return [list(pair) for pair in zip(*made)]

    def exchange(pair):
        return [swap(pair[r], r) for r in ROLES]

    wb, i1b, s1 = [None, None], [None, None], [None, None]
    for r in (1, 0):
        given = [(m_edge, one), (w_edge, one)] + tdt + [(mr[r], one), (th[r], whole)] + side(r, w_in, i1_in)
        wb[r], i1b[r], s1[r] = call(outer_1(r), info, given, [out(3, 2), out(2), out(2)], [slopes], 3)
        if r == 1:
            mr[0], s1[1] = lax.optimization_barrier((mr[0], s1[1]))
    r1 = exchange(s1)
    i3_in, i4_in, a4_in = call(
        inner_2,
        info,
        [(w_in, one), (i2_in, one)] + both(s1, one) + [(targets, one)],
        [out(6), out(4), out(4)],
        [planes(8)],
        us=4,
    )
    i3b, i4b, a4b, s2 = sides(
        outer_2, lambda r: [(targets, one)], [r1, wb, w_in, s1, i3_in], [out(2), out(2), out(1), out(2)], [], 2, waits=0
    )
    r2 = exchange(s2)
    a3_in, a2_in, g_in, warped = call(
        inner_3,
        info,
        [(w_in, one)]
        + both(wb, one)
        + both(s2, one)
        + both(a4b, one)
        + [(a4_in, one), (i3_in, one)]
        + both(i3b, one)
        + [(i2_in, one)]
        + both(s1, one)
        + [(i1_in, one), (i4_in, one)]
        + both(i4b, one),
        [out(6), out(4), out(3, 6), (shape(8), None)],
        [planes(8)] * 3 + [pltpu.SemaphoreType.DMA((8,))],
        us=7,
    )
    images = [i3b, i3_in, r1, s1, i1b, i1_in]
    a3b, a2b, s3 = sides(
        outer_3, lambda r: [], [r2, wb, w_in, s2, a3_in] + images, [out(2), out(2), out(3)], [], 2, waits=0
    )
    r3 = exchange(s3)
    small, six, tile = ((groups, n, 8, COLS) for n in (4, 6, 8))
    a1_in, total, g_full, *gb = call(
        inner_4,
        info,
        [(w_in, one)]
        + both(wb, one)
        + [(a2_in, one)]
        + both(a2b, one)
        + both(r2, one)
        + both(a3b, one)
        + both(s2, one)
        + both(s3, one)
        + both(i3b, one)
        + near(i3_in)
        + both(r1, one)
        + both(s1, one)
        + both(i1b, one)
        + near(i1_in)
        + tdt
        + [(g_in, one)],
        [out(6), (small, whole), out(3, 6)] + out2(3, 2),
        [planes(8)] * 2,
        us=5,
    )
    a1b = [None, None]
    for r in (1, 0):
        total, a1b[r] = call(
            outer_4(r),
            info,
            side(r, r3, wb, w_in, s3, a1_in) + [(total, whole)],
            [(six, whole) if r else (tile, None), (shape(2), None)],
            [pltpu.VMEM((groups, 2, 8, COLS), f32), pltpu.VMEM((4, 2) + PLANE, f32), pltpu.SemaphoreType.DMA((6,))],
            2,
        )
        if r == 1:
            r3[0], total = lax.optimization_barrier((r3[0], total))
    parts = lax.all_to_all(total, "subj", 0, 0)
    (momentum_gradient,) = call(
        finish,
        info,
        both(r3, stream) + both(a1b, stream) + both(gb, stream) + both(i1b, stream) + both(th, whole) + tdt + [(g_full, stream)],
        [(shape(3, 8), None)],
        [pltpu.VMEM((2, 3, 8) + PLANE, f32), pltpu.SemaphoreType.DMA((2,)), slopes],
        us=6,
        mib=14,
    )
    template_gradient = jnp.sum(parts, axis=0)
    return (warped, template_gradient, momentum_gradient)


def solution(mesh):
    in_specs = (
        P("space", "subj", None),
        P("subj", None, "space", None, None),
        P("subj", "space", None, None),
        P("subj"),
    )
    out_specs = (
        P("subj", "space", None, None),
        P("space", "subj", None),
        P("subj", None, "space", None, None),
    )
    return jax.shard_map(shards, mesh=mesh, in_specs=in_specs, out_specs=out_specs, check_vma=False)
```
